32 devices in a mesh: dp: 8 (over y, x, core), seq: 4 (over z).
Axes of the slice: x: 2, y: 2, z: 4, core: 2. Of those that a mesh axis runs over, the one named last changes fastest.
Arguments:
- queries: bfloat16 [16384, 1536], P(('dp', 'seq')), may hold values from -8 to 8
- keys: bfloat16 [16384, 1536], P(('dp', 'seq')), may hold values from -8 to 8
- values: bfloat16 [16384, 1536], P(('dp', 'seq')), may hold values from -6 to 6
- grad_out: bfloat16 [16384, 1536], P(('dp', 'seq')), may hold values from -6 to 6
- out_weight: bfloat16 [1536, 1536], P('dp'), may hold values from -0.15625 to 0.15625
- lengths: int32 [8], P('dp'), may hold values from 256 to 2048, as said below
Outputs:
- grad_queries: bfloat16 [16384, 1536], P(('dp', 'seq'))
- grad_keys: bfloat16 [16384, 1536], P(('dp', 'seq'))
- grad_values: bfloat16 [16384, 1536], P(('dp', 'seq'))
- grad_weight: float32 [1536, 1536], P(('dp', 'seq'))
The draws below stay inside these ranges and needn't reach their ends.
Inputs may be any that keep to these rules, and one draw needn't show every extreme that they name: `lengths`: every draw holds one stretch of 2048 valid bytes and one of 256.
All inputs are finite; a program needn't handle non-finite values.
Results may differ from the reference program's by a relative error of at most 0.0058.
Values may be sent and summed in bfloat16 or wider, within the bound.
A program may use at most 192 MiB of HBM per device.

```python
import jax
import jax.numpy as jnp
from jax import lax

HEADS = 12
HEAD_DIM = 128
D = 1536
WINDOW = 512
TOK_DEV = 512
DOC = 2048
DOCS = 8
TOKENS = 16384


def drawn_pair(base_key):
    seeded = jax.random.fold_in(base_key, 11)
    key_query, key_keys = jax.random.split(seeded, 2)
    query_vals = jax.random.normal(key_query, (TOKENS, D), jnp.float32)
    key_vals = jax.random.normal(key_keys, (TOKENS, D), jnp.float32)
    return (jnp.clip(query_vals, -8.0, 8.0), jnp.clip(key_vals, -8.0, 8.0))


def draw_queries(key, part):
    return drawn_pair(key)[0].astype(jnp.bfloat16)


def draw_keys(key, part):
    return drawn_pair(key)[1].astype(jnp.bfloat16)


def draw_lengths(key, part):
    key_base, key_order = jax.random.split(jax.random.fold_in(key, 23))
    drawn = jax.random.randint(key_base, (DOCS,), DOC // 8, DOC + 1)
    order = jax.random.permutation(key_order, DOCS)
    drawn = drawn.at[order[0]].set(DOC)
    drawn = drawn.at[order[1]].set(DOC // 8)
    return drawn.astype(jnp.int32)


def strengthened(values, rng, source, target, parts, factor):
    owner, partner = [(jnp.arange(values.shape[dim]) // (values.shape[dim] // parts)).reshape([-1 if axis == dim else 1 for axis in range(values.ndim)]) for dim in (source, target)]
    chosen = jax.random.permutation(rng, parts)[partner]
    strong = (owner == chosen) | (owner == (partner + parts // 2) % parts)
    return jnp.where(strong, factor * values, values)


def levels(stream_key, dims, cuts, low, largest):
    def one(dim, parts):
        steps = jax.random.uniform(jax.random.fold_in(jax.random.fold_in(stream_key, 6), dim), (parts,), jnp.float32, low / len(cuts), largest / len(cuts))
        return jnp.repeat(jnp.exp(steps), dims[dim] // parts).reshape((-1,) + (1,) * (len(dims) - dim - 1))

    loudness = one(*cuts[0])
    for cut in cuts[1:]:
        loudness = loudness * one(*cut)
    return loudness


def bell_draw(own_key, shape, scale, limit, shards=(), kind=jnp.bfloat16):
    values = jax.random.normal(own_key, shape, jnp.float32) * scale
    if len(shards) > 0:
        values = levels(own_key, shape, shards, -0.22, 0.18) * values
    return jnp.clip(values, min=-limit, max=limit).astype(kind)


def heavy_noise(stream_key, extent, spread, reach, pieces, heavy, kind=jnp.bfloat16):
    values = spread * jax.random.normal(stream_key, extent, jnp.float32)
    if pieces:
        values = values * levels(stream_key, extent, pieces, -0.22, 0.18)
    return jnp.clip(strengthened(values, jax.random.fold_in(stream_key, 3), *heavy), -reach, reach).astype(kind)


def setup_inputs(seed: int = 0) -> dict:
    key_list = jax.random.split(jax.random.key(seed), 7)
    return {
        "queries": draw_queries(jax.random.fold_in(key_list[6], 71), 0),
        "keys": draw_keys(jax.random.fold_in(key_list[6], 71), 0),
        "values": bell_draw(key_list[2], (TOKENS, D), 1.0, 6.0, ((0, 32),)),
        "grad_out": heavy_noise(key_list[3], (TOKENS, D), 1.0, 6.0, ((0, 32),), (0, 1, 32, 2.75)),
        "out_weight": bell_draw(key_list[4], (D, D), D ** -0.5, 0.15625, ((0, 8),)),
        "lengths": draw_lengths(jax.random.fold_in(key_list[6], 71), 0),
    }


def window_backward(query_block, key_window, value_window, grad_block, query_pos, key_pos, length):
    half_window = WINDOW // 2
    inv_root = HEAD_DIM ** -0.5
    offset = key_pos[None, :] - query_pos[:, None]
    allowed = (offset >= -half_window) & (offset < half_window)
    allowed = allowed & (key_pos[None, :] >= 0) & (key_pos[None, :] < length) & (query_pos[:, None] < length)

    def split_heads(matrix):
        return matrix.reshape(matrix.shape[0], HEADS, HEAD_DIM).transpose(1, 0, 2)

    def join_heads(stacked):
        return stacked.transpose(1, 0, 2).reshape(stacked.shape[1], HEADS * HEAD_DIM)

    def one_head(operands):
        query_head, key_head, value_head, grad_head = operands
        scores = lax.dot_general(query_head, key_head, (((1,), (1,)), ((), ())), preferred_element_type=jnp.float32) * inv_root
        scores = jnp.where(allowed, scores, -1e30)
        row_max = jnp.max(scores, axis=1, keepdims=True)
        expo = jnp.where(allowed, jnp.exp(scores - row_max), 0.0)
        row_total = jnp.maximum(jnp.sum(expo, axis=1, keepdims=True), 1.0)
        probability = expo / row_total
        probability_b = probability.astype(jnp.bfloat16)
        attended_head = jnp.dot(probability_b, value_head, preferred_element_type=jnp.float32)
        grad_probs = lax.dot_general(grad_head, value_head, (((1,), (1,)), ((), ())), preferred_element_type=jnp.float32)
        row_delta = jnp.sum(probability * grad_probs, axis=1, keepdims=True)
        grad_scores = (probability * (grad_probs - row_delta) * inv_root).astype(jnp.bfloat16)
        grad_query = jnp.dot(grad_scores, key_head, preferred_element_type=jnp.float32)
        grad_key = lax.dot_general(grad_scores, query_head, (((0,), (0,)), ((), ())), preferred_element_type=jnp.float32)
        grad_value = lax.dot_general(probability_b, grad_head, (((0,), (0,)), ((), ())), preferred_element_type=jnp.float32)
        return attended_head, grad_query, grad_key, grad_value

    outputs = lax.map(one_head, (split_heads(query_block), split_heads(key_window), split_heads(value_window), split_heads(grad_block)))
    attended_heads, grad_query, grad_key, grad_value = outputs
    return join_heads(attended_heads).astype(jnp.bfloat16), join_heads(grad_query), join_heads(grad_key), join_heads(grad_value)


def reference(queries, keys, values, grad_out, out_weight, lengths):
    half_window = WINDOW // 2
    block_count = DOC // TOK_DEV
    window_rows = TOK_DEV + 2 * half_window

    def single_document(operands):
        doc_query, doc_keys, doc_values, doc_grad, length = operands
        grad_mixed = jnp.dot(doc_grad, out_weight, preferred_element_type=jnp.float32).astype(jnp.bfloat16)
        zero_rows = jnp.zeros((half_window, D), jnp.bfloat16)
        keys_padded = jnp.concatenate([zero_rows, doc_keys, zero_rows], axis=0)
        values_padded = jnp.concatenate([zero_rows, doc_values, zero_rows], axis=0)

        def block_step(accumulator, block_index):
            first_row = (block_index * TOK_DEV).astype(jnp.int32)
            query_block = lax.dynamic_slice_in_dim(doc_query, first_row, TOK_DEV, 0)
            key_window = lax.dynamic_slice_in_dim(keys_padded, first_row, window_rows, 0)
            value_window = lax.dynamic_slice_in_dim(values_padded, first_row, window_rows, 0)
            grad_block = lax.dynamic_slice_in_dim(grad_mixed, first_row, TOK_DEV, 0)
            query_pos = first_row + jnp.arange(TOK_DEV, dtype=jnp.int32)
            key_pos = first_row - half_window + jnp.arange(window_rows, dtype=jnp.int32)
            attended, grad_query, grad_key, grad_value = window_backward(query_block, key_window, value_window, grad_block, query_pos, key_pos, length)
            paired = jnp.stack([grad_key, grad_value])
            current = lax.dynamic_slice_in_dim(accumulator, first_row, window_rows, 1)
            accumulator = lax.dynamic_update_slice_in_dim(accumulator, current + paired, first_row, 1)
            return accumulator, (attended, grad_query)

        start_acc = jnp.zeros((2, DOC + 2 * half_window, D), jnp.float32)
        accumulator, (attended, grad_query) = lax.scan(block_step, start_acc, jnp.arange(block_count, dtype=jnp.int32))
        attended = attended.reshape(DOC, D)
        grad_query = grad_query.reshape(DOC, D).astype(jnp.bfloat16)
        key_value = accumulator[:, half_window:half_window + DOC].astype(jnp.bfloat16)
        weight_part = lax.dot_general(doc_grad, attended, (((0,), (0,)), ((), ())), preferred_element_type=jnp.float32)
        return grad_query, key_value[0], key_value[1], weight_part

    def shaped(matrix):
        return matrix.reshape(DOCS, DOC, D)

    grad_query, grad_key, grad_value, weight_parts = lax.map(single_document, (shaped(queries), shaped(keys), shaped(values), shaped(grad_out), lengths))
    return (grad_query.reshape(TOKENS, D), grad_key.reshape(TOKENS, D), grad_value.reshape(TOKENS, D), jnp.sum(weight_parts, axis=0))
```

```python
import functools

import jax
import jax.numpy as jnp
from jax import lax
from jax.experimental import pallas as pl
from jax.experimental.pallas import tpu as pltpu
from jax.sharding import PartitionSpec as P

HEADS = 12
HEAD_DIM = 128
WINDOW = 512
HALF = WINDOW // 2
GROUP = 2
COLS = GROUP * HEAD_DIM
BLOCK = HALF
INV_ROOT = HEAD_DIM ** (-0.5)
LOG2E = 1.4426950408889634
NT = (((1,), (1,)), ((), ()))
NN = (((1,), (0,)), ((), ()))
TN = (((0,), (0,)), ((), ()))


def mm(a, b, dims):
    return lax.dot_general(a, b, dims, preferred_element_type=jnp.float32)


def fill_bias(bias, length, first_row):
    for i in range(bias.shape[0]):
        shape = (BLOCK + 2 * HALF, BLOCK)
        key = lax.broadcasted_iota(jnp.int32, shape, 0)
        query = lax.broadcasted_iota(jnp.int32, shape, 1)
        key_pos = first_row + (i * BLOCK - HALF) + key
        allowed = (key >= query) & (key < query + WINDOW) & (key_pos >= 0) & (key_pos < length)
        bias[i] = jnp.where(allowed, 0.0, -1e30)


def attend(q_ref, cols, kx, vx, g, bias, att, gq_ref, gk_acc, gv_acc, length, first_row):
    blocks = bias.shape[0]
    span = BLOCK + 2 * HALF
    for hh in range(GROUP):
        hc = slice(hh * HEAD_DIM, (hh + 1) * HEAD_DIM)
        for i in range(blocks):
            rows = slice(i * BLOCK, (i + 1) * BLOCK)
            win = slice(i * BLOCK, i * BLOCK + span)
            qh = q_ref[rows, cols][:, hc]
            gh = g[rows, hc]
            kw = kx[win, hc]
            vw = vx[win, hc]
            t = mm(kw, qh, NT) * (INV_ROOT * LOG2E) + bias[i]
            top = jnp.max(t, axis=0, keepdims=True)
            e = jnp.exp2(t - top)
            total = jnp.maximum(jnp.sum(e, axis=0, keepdims=True), 1.0)
            pos = first_row + i * BLOCK + lax.broadcasted_iota(jnp.int32, (1, BLOCK), 1)
            p = e * jnp.where(pos < length, 1.0 / total, 0.0)
            pb = p.astype(jnp.bfloat16)
            att[hc, rows] = mm(vw, pb, TN).astype(jnp.bfloat16)
            dp = mm(vw, gh, NT)
            delta = jnp.sum(p * dp, axis=0, keepdims=True)
            gs = (p * (dp - delta)).astype(jnp.bfloat16)
            gq = (mm(kw, gs, TN) * INV_ROOT).T
            gq_ref[rows, pl.ds(cols.start + hh * HEAD_DIM, HEAD_DIM)] = gq.astype(jnp.bfloat16)
            gk = mm(gs, qh, NN) * INV_ROOT
            gv = mm(pb, gh, NN)
            for acc, new in ((gk_acc, gk), (gv_acc, gv)):
                if i == 0:
                    acc[win, hc] = new
                else:
                    old = slice(i * BLOCK, i * BLOCK + 2 * HALF)
                    acc[old, hc] += new[: 2 * HALF]
                    acc[i * BLOCK + 2 * HALF : i * BLOCK + span, hc] = new[2 * HALF :]


def kernel(
    len_ref, q_ref, k_ref, v_ref, go_ref, w_ref, low_ref, high_ref,
    gq_ref, own_ref, rim_ref, wg_ref,
    bias, got, kx, vx, g, att, gk_acc, gv_acc,
):
    tok = q_ref.shape[0]
    first_row = lax.axis_index("seq") * tok
    length = len_ref[0]
    fill_bias(bias, length, first_row)
    got[...] = go_ref[...].T

    def step(n, carry):
        cols = pl.ds(pl.multiple_of(n * COLS, COLS), COLS)
        for s, (x, ref) in enumerate(((kx, k_ref), (vx, v_ref))):
            x[:HALF] = low_ref[s, :, cols]
            x[HALF : HALF + tok] = ref[:, cols]
            x[HALF + tok :] = high_ref[s, :, cols]
        g[...] = mm(go_ref[...], w_ref[:, cols], NN).astype(jnp.bfloat16)
        attend(q_ref, cols, kx, vx, g, bias, att, gq_ref, gk_acc, gv_acc, length, first_row)
        for s, acc in enumerate((gk_acc, gv_acc)):
            rim_ref[0, s, :, cols] = acc[:HALF].astype(jnp.bfloat16)
            own_ref[s, :, cols] = acc[HALF : HALF + tok]
            rim_ref[1, s, :, cols] = acc[HALF + tok :].astype(jnp.bfloat16)
        wg_ref[:, cols] = mm(got[...], att[...], NT)
        return carry

    lax.fori_loop(0, q_ref.shape[1] // COLS, step, 0)


def passed_along(value, axis, by):
    devices = lax.axis_size(axis)
    pairs = [(i, i + by) for i in range(devices) if 0 <= i + by < devices]
    return lax.ppermute(value, axis, pairs)


def shards(queries, keys, values, grad_out, out_weight, lengths):
    tok, width = queries.shape
    stacked = jnp.stack([keys, values])
    low = passed_along(stacked[:, tok - HALF :], "seq", 1)
    high = passed_along(stacked[:, :HALF], "seq", -1)
    weight = lax.all_gather(out_weight, "dp", axis=0, tiled=True)
    vmem = pl.BlockSpec(memory_space=pltpu.VMEM)
    smem = pl.BlockSpec(memory_space=pltpu.SMEM)
    bf, f32 = jnp.bfloat16, jnp.float32
    grad_query, own, rim, partial = pl.pallas_call(
        kernel,
        out_shape=(
            jax.ShapeDtypeStruct((tok, width), bf),
            jax.ShapeDtypeStruct((2, tok, width), f32),
            jax.ShapeDtypeStruct((2, 2, HALF, width), bf),
            jax.ShapeDtypeStruct((weight.shape[0], width), f32),
        ),
        in_specs=[smem] + [vmem] * 7,
        out_specs=(vmem,) * 4,
        scratch_shapes=[
            pltpu.VMEM((tok // BLOCK, BLOCK + 2 * HALF, BLOCK), f32),
            pltpu.VMEM((weight.shape[0], tok), bf),
            pltpu.VMEM((tok + 2 * HALF, COLS), bf),
            pltpu.VMEM((tok + 2 * HALF, COLS), bf),
            pltpu.VMEM((tok, COLS), bf),
            pltpu.VMEM((COLS, tok), bf),
            pltpu.VMEM((tok + 2 * HALF, COLS), f32),
            pltpu.VMEM((tok + 2 * HALF, COLS), f32),
        ],
        compiler_params=pltpu.CompilerParams(vmem_limit_bytes=60 * 1024 * 1024),
        cost_estimate=pl.CostEstimate(
            flops=20_000_000_000, bytes_accessed=30_000_000, transcendentals=5_000_000
        ),
    )(lengths, queries, keys, values, grad_out, weight, low, high)
    from_right = passed_along(rim[0], "seq", -1)
    from_left = passed_along(rim[1], "seq", 1)
    own = own.at[:, :HALF].add(from_left.astype(f32))
    own = own.at[:, tok - HALF :].add(from_right.astype(f32))
    weight_grad = lax.psum_scatter(partial, "dp", scatter_dimension=0, tiled=True)
    weight_grad = lax.psum_scatter(weight_grad, "seq", scatter_dimension=0, tiled=True)
    return grad_query, own[0].astype(bf), own[1].astype(bf), weight_grad


def solution(mesh):
    rows = P(("dp", "seq"), None)
    in_specs = (rows, rows, rows, rows, P("dp", None), P("dp"))
    return jax.shard_map(
        shards, mesh=mesh, in_specs=in_specs, out_specs=(rows,) * 4, check_vma=False
    )
```

```python
import functools

import jax
import jax.numpy as jnp
from jax import lax
from jax.experimental import pallas as pl
from jax.experimental.pallas import tpu as pltpu
from jax.sharding import PartitionSpec as P

HEADS = 12
HEAD_DIM = 128
WINDOW = 512
HALF = WINDOW // 2
GROUP = 2
COLS = GROUP * HEAD_DIM
BLOCK = HALF
INV_ROOT = HEAD_DIM ** (-0.5)
LOG2E = 1.4426950408889634
NT = (((1,), (1,)), ((), ()))
NN = (((1,), (0,)), ((), ()))
TN = (((0,), (0,)), ((), ()))


def mm(a, b, dims):
    return lax.dot_general(a, b, dims, preferred_element_type=jnp.float32)


def fill_bias(bias, length, first_row):
    for i in range(bias.shape[0]):
        shape = (BLOCK + 2 * HALF, BLOCK)
        key = lax.broadcasted_iota(jnp.int32, shape, 0)
        query = lax.broadcasted_iota(jnp.int32, shape, 1)
        key_pos = first_row + (i * BLOCK - HALF) + key
        allowed = (key >= query) & (key < query + WINDOW) & (key_pos >= 0) & (key_pos < length)
        bias[i] = jnp.where(allowed, 0.0, -1e30)


def attend(q_ref, cols, kx, vx, g, bias, att, gq_ref, gk_acc, gv_acc, length, first_row):
    blocks = bias.shape[0]
    span = BLOCK + 2 * HALF
    for hh in range(GROUP):
        hc = slice(hh * HEAD_DIM, (hh + 1) * HEAD_DIM)
        for i in range(blocks):
            rows = slice(i * BLOCK, (i + 1) * BLOCK)
            win = slice(i * BLOCK, i * BLOCK + span)
            qh = q_ref[rows, cols][:, hc]
            gh = g[rows, hc]
            kw = kx[win, hc]
            vw = vx[win, hc]
            t = mm(kw, qh, NT) * (INV_ROOT * LOG2E) + bias[i]
            top = jnp.max(t, axis=0, keepdims=True)
            e = jnp.exp2(t - top)
            total = jnp.maximum(jnp.sum(e, axis=0, keepdims=True), 1.0)
            pos = first_row + i * BLOCK + lax.broadcasted_iota(jnp.int32, (1, BLOCK), 1)
            p = e * jnp.where(pos < length, 1.0 / total, 0.0)
            pb = p.astype(jnp.bfloat16)
            att[hc, rows] = mm(vw, pb, TN).astype(jnp.bfloat16)
            dp = mm(vw, gh, NT)
            delta = jnp.sum(p * dp, axis=0, keepdims=True)
            gs = (p * (dp - delta)).astype(jnp.bfloat16)
            gq = (mm(kw, gs, TN) * INV_ROOT).T
            gq_ref[rows, pl.ds(cols.start + hh * HEAD_DIM, HEAD_DIM)] = gq.astype(jnp.bfloat16)
            gk = mm(gs, qh, NN) * INV_ROOT
            gv = mm(pb, gh, NN)
            for acc, new in ((gk_acc, gk), (gv_acc, gv)):
                if i == 0:
                    acc[win, hc] = new
                else:
                    old = slice(i * BLOCK, i * BLOCK + 2 * HALF)
                    acc[old, hc] += new[: 2 * HALF]
                    acc[i * BLOCK + 2 * HALF : i * BLOCK + span, hc] = new[2 * HALF :]


def ring_add(index, by, count):
    return lax.rem(index + by, count)


def kernel(
    count, seq, len_ref, q_ref, k_ref, v_ref, go_ref, w_ref,
    gq_ref, gk_ref, gv_ref, wg_ref,
    bias, got, kx, vx, g, att, gk_acc, gv_acc,
    w_all, halo, rim, own, part, fin, piece, piece_in,
    keeps, sends, recvs,
    w_send, w_recv, w_pass, halo_send, halo_recv, rim_send, rim_recv,
    red_send, red_recv, piece_send, piece_recv,
):
    tok, width = q_ref.shape
    groups = width // COLS
    chips = count // 2
    stages = len(keeps)
    depth = w_ref.shape[0]
    dp, z = lax.axis_index("dp"), lax.axis_index("seq")
    chip, core = lax.div(dp, 2), lax.rem(dp, 2)
    sibling = dp + 1 - 2 * core
    first_row = z * tok
    length = len_ref[0]
    rows_out = wg_ref.shape[0]
    split_seq = rows_out != depth

    def copy(source, target, send_sem, recv_sem, to_dp, to_z):
        return pltpu.make_async_remote_copy(
            src_ref=source, dst_ref=target, send_sem=send_sem, recv_sem=recv_sem,
            device_id=(to_dp, to_z), device_id_type=pl.DeviceIdType.MESH,
        )

    def columns(n):
        return pl.ds(pl.multiple_of(n * COLS, COLS), COLS)

    def same_core(d):
        return 2 * ring_add(chip, d, chips) + core

    def weight_copy(n, d):
        to = sibling if d == 0 else same_core(d)
        return copy(w_ref.at[:, columns(n)], w_all.at[n, dp], w_send.at[n, d], w_recv.at[n, dp], to, z)

    def weight_from(n, block, to):
        return copy(w_all.at[n, block], w_all.at[n, block], w_pass.at[n, 0], w_recv.at[n, block], to, z)

    def weight_pass(n, d):
        block = same_core(d)
        return copy(
            w_all.at[n, block], w_all.at[n, block], w_pass.at[n, d], w_recv.at[n, block], sibling, z
        )

    def halo_copy(n, side, s):
        ref = (k_ref, v_ref)[s]
        start = tok - HALF if side == 0 else 0
        return copy(
            ref.at[pl.ds(start, HALF), columns(n)], halo.at[side, s, n],
            halo_send.at[side, s, n], halo_recv.at[side, s, n], dp, z + 1 - 2 * side,
        )

    def rim_copy(n, side, s):
        return copy(
            halo.at[side, s, n], rim.at[1 - side, s, n],
            rim_send.at[side, s, n], rim_recv.at[1 - side, s, n], dp, z - 1 + 2 * side,
        )

    def reduce_copy(s, n):
        bit = lax.rem(lax.div(dp, 2**s), 2)
        return copy(
            sends[s].at[n], recvs[s].at[n], red_send.at[s, n], red_recv.at[s, n],
            dp + (1 - 2 * bit) * 2**s, z,
        )

    def piece_copy(n, d):
        to = ring_add(z, d, seq)
        rows = pl.ds(pl.multiple_of(to * rows_out, 16), rows_out)
        return copy(
            piece.at[n, rows], piece_in.at[n, z], piece_send.at[n, d], piece_recv.at[n, z], dp, to
        )

    def piece_from(n, d):
        block = ring_add(z, d, seq)
        rows = pl.ds(pl.multiple_of(block * rows_out, 16), rows_out)
        return copy(
            piece.at[n, rows], piece_in.at[n, block], piece_send.at[n, d], piece_recv.at[n, block],
            dp, block,
        )

    has_before, has_after = z > 0, z < seq - 1
    exists = (has_before, has_after)

    barrier = pltpu.get_barrier_semaphore()
    peers = [(sibling, z)]
    peers += [(same_core(d), z) for d in range(1, chips)]
    peers += [(dp, ring_add(z, d, seq)) for d in range(1, seq)]
    for peer in peers:
        pl.semaphore_signal(barrier, inc=1, device_id=peer, device_id_type=pl.DeviceIdType.MESH)
    pl.semaphore_wait(barrier, len(peers))

    def begin(n, carry):
        for d in range(chips):
            weight_copy(n, d).start()
        for side in range(2):
            @pl.when(exists[1 - side])
            def _():
                for s in range(2):
                    halo_copy(n, side, s).start()
        w_all[n, dp] = w_ref[:, columns(n)]
        return carry

    lax.fori_loop(0, groups, begin, 0)
    for side in range(2):
        @pl.when(jnp.logical_not(exists[side]))
        def _():
            halo[side] = jnp.zeros(halo.shape[1:], halo.dtype)

    fill_bias(bias, length, first_row)
    got[...] = go_ref[...].T

    def pass_weight(n):
        for d in range(1, chips):
            weight_from(n, same_core(d), sibling).wait_recv()
            weight_pass(n, d).start()

    def reduce_stage(s, n):
        slot = lax.rem(n, 2)
        if s > 0:
            reduce_copy(s - 1, n).wait_recv()

        def held(i):
            if s == 0:
                return part[i]
            return keeps[s - 1][slot, i] + recvs[s - 1][n, i].astype(jnp.float32)

        if s == stages:
            fin[n] = held(0)
            if split_seq:
                piece[n] = fin[n].astype(jnp.bfloat16)
                for d in range(1, seq):
                    piece_copy(n, d).start()
            return
        bit = lax.rem(lax.div(dp, 2**s), 2)
        for i in range(keeps[s].shape[1]):
            sends[s][n, i] = held(2 * i + 1 - bit).astype(jnp.bfloat16)
            keeps[s][slot, i] = held(2 * i + bit)
        reduce_copy(s, n).start()

    def advance(n):
        for s in range(stages, 0, -1):
            @pl.when((n >= s) & (n - s < groups))
            def _():
                reduce_stage(s, n - s)

    pass_weight(0)

    def step(n, carry):
        cols = columns(n)
        for d in range(chips):
            weight_from(n, same_core(d) + 1 - 2 * core, sibling).wait_recv()
        weight = w_all[n].reshape(count * depth, COLS)
        g[...] = mm(go_ref[...], weight, NN).astype(jnp.bfloat16)
        for side in range(2):
            @pl.when(exists[side])
            def _():
                for s in range(2):
                    halo_copy(n, side, s).wait_recv()
        for s, (x, ref) in enumerate(((kx, k_ref), (vx, v_ref))):
            x[:HALF] = halo[0, s, n]
            x[HALF : HALF + tok] = ref[:, cols]
            x[HALF + tok :] = halo[1, s, n]
        attend(q_ref, cols, kx, vx, g, bias, att, gq_ref, gk_acc, gv_acc, length, first_row)
        for s, acc in enumerate((gk_acc, gv_acc)):
            halo[0, s, n] = acc[:HALF].astype(jnp.bfloat16)
            halo[1, s, n] = acc[HALF + tok :].astype(jnp.bfloat16)
            own[s, n] = acc[HALF : HALF + tok]
        for side in range(2):
            @pl.when(exists[side])
            def _():
                for s in range(2):
                    rim_copy(n, side, s).start()

        @pl.when(n + 1 < groups)
        def _():
            pass_weight(n + 1)

        advance(n)
        part[...] = mm(got[...], att[...], NT).reshape(part.shape)
        reduce_stage(0, n)
        return carry

    lax.fori_loop(0, groups, step, 0)

    def drain(n, carry):
        advance(n)
        return carry

    lax.fori_loop(groups, groups + stages, drain, 0)

    def finish(n, carry):
        cols = columns(n)
        for side in range(2):
            rows = pl.ds(0 if side == 0 else tok - HALF, HALF)

            @pl.when(exists[side])
            def _():
                for s in range(2):
                    rim_copy(n, 1 - side, s).wait_recv()
                    own[s, n, rows] += rim[side, s, n].astype(jnp.float32)

        gk_ref[:, cols] = own[0, n].astype(jnp.bfloat16)
        gv_ref[:, cols] = own[1, n].astype(jnp.bfloat16)
        if split_seq:
            total = fin[n, pl.ds(pl.multiple_of(z * rows_out, 16), rows_out)]
            for d in range(1, seq):
                piece_from(n, d).wait_recv()
                total += piece_in[n, ring_add(z, d, seq)].astype(jnp.float32)
            wg_ref[:, cols] = total
        else:
            wg_ref[:, cols] = fin[n]
        for d in range(chips):
            weight_copy(n, d).wait_send()
        for d in range(1, chips):
            weight_pass(n, d).wait_send()
        for side in range(2):
            @pl.when(exists[1 - side])
            def _():
                for s in range(2):
                    halo_copy(n, side, s).wait_send()

            @pl.when(exists[side])
            def _():
                for s in range(2):
                    rim_copy(n, side, s).wait_send()
        for s in range(stages):
            reduce_copy(s, n).wait_send()
        if split_seq:
            for d in range(1, seq):
                piece_copy(n, d).wait_send()
        return carry

    lax.fori_loop(0, groups, finish, 0)


def shards(queries, keys, values, grad_out, out_weight, lengths):
    tok, width = queries.shape
    depth = out_weight.shape[0]
    count, seq = lax.axis_size("dp"), lax.axis_size("seq")
    stages = count.bit_length() - 1
    groups = width // COLS
    wide = tok + 2 * HALF
    split_seq = seq > 1 and (depth // seq) % 16 == 0
    rows_out = depth // seq if split_seq else depth
    vmem = pl.BlockSpec(memory_space=pltpu.VMEM)
    smem = pl.BlockSpec(memory_space=pltpu.SMEM)
    bf, f32 = jnp.bfloat16, jnp.float32
    dma = pltpu.SemaphoreType.DMA
    halves = [count >> (s + 1) for s in range(stages)]
    grad_query, grad_key, grad_value, weight_grad = pl.pallas_call(
        functools.partial(kernel, count, seq),
        out_shape=(
            jax.ShapeDtypeStruct((tok, width), bf),
            jax.ShapeDtypeStruct((tok, width), bf),
            jax.ShapeDtypeStruct((tok, width), bf),
            jax.ShapeDtypeStruct((rows_out, width), f32),
        ),
        in_specs=[smem] + [vmem] * 5,
        out_specs=(vmem,) * 4,
        scratch_shapes=[
            pltpu.VMEM((tok // BLOCK, BLOCK + 2 * HALF, BLOCK), f32),
            pltpu.VMEM((width, tok), bf),
            pltpu.VMEM((wide, COLS), bf),
            pltpu.VMEM((wide, COLS), bf),
            pltpu.VMEM((tok, COLS), bf),
            pltpu.VMEM((COLS, tok), bf),
            pltpu.VMEM((wide, COLS), f32),
            pltpu.VMEM((wide, COLS), f32),
            pltpu.VMEM((groups, count, depth, COLS), bf),
            pltpu.VMEM((2, 2, groups, HALF, COLS), bf),
            pltpu.VMEM((2, 2, groups, HALF, COLS), bf),
            pltpu.VMEM((2, groups, tok, COLS), f32),
            pltpu.VMEM((count, depth, COLS), f32),
            pltpu.VMEM((groups, depth, COLS), f32),
            pltpu.VMEM((groups, depth, COLS), bf),
            pltpu.VMEM((groups, seq, depth // seq if split_seq else 16, COLS), bf),
            [pltpu.VMEM((2, h, depth, COLS), f32) for h in halves],
            [pltpu.VMEM((groups, h, depth, COLS), bf) for h in halves],
            [pltpu.VMEM((groups, h, depth, COLS), bf) for h in halves],
            dma((groups, count // 2)),
            dma((groups, count)),
            dma((groups, count // 2)),
            dma((2, 2, groups)),
            dma((2, 2, groups)),
            dma((2, 2, groups)),
            dma((2, 2, groups)),
            dma((stages, groups)),
            dma((stages, groups)),
            dma((groups, seq)),
            dma((groups, seq)),
        ],
        compiler_params=pltpu.CompilerParams(
            vmem_limit_bytes=62 * 1024 * 1024, collective_id=0, has_side_effects=True
        ),
        cost_estimate=pl.CostEstimate(
            flops=20_000_000_000, bytes_accessed=12_000_000, transcendentals=5_000_000
        ),
    )(lengths, queries, keys, values, grad_out, out_weight)
    if not split_seq:
        weight_grad = lax.psum_scatter(weight_grad, "seq", scatter_dimension=0, tiled=True)
    return grad_query, grad_key, grad_value, weight_grad


def solution(mesh):
    rows = P(("dp", "seq"), None)
    in_specs = (rows, rows, rows, rows, P("dp", None), P("dp"))
    return jax.shard_map(
        shards, mesh=mesh, in_specs=in_specs, out_specs=(rows,) * 4, check_vma=False
    )
```

```python
import functools

import jax
import jax.numpy as jnp
from jax import lax
from jax.experimental import pallas as pl
from jax.experimental.pallas import tpu as pltpu
from jax.sharding import PartitionSpec as P

HEADS = 12
HEAD_DIM = 128
WINDOW = 512
HALF = WINDOW // 2
GROUP = 2
COLS = GROUP * HEAD_DIM
BLOCK = HALF
INV_ROOT = HEAD_DIM ** (-0.5)
LOG2E = 1.4426950408889634
NT = (((1,), (1,)), ((), ()))
NN = (((1,), (0,)), ((), ()))
TN = (((0,), (0,)), ((), ()))


def mm(a, b, dims):
    return lax.dot_general(a, b, dims, preferred_element_type=jnp.float32)


def fill_bias(bias, length, first_row):
    for i in range(bias.shape[0]):
        shape = (BLOCK + 2 * HALF, BLOCK)
        key = lax.broadcasted_iota(jnp.int32, shape, 0)
        query = lax.broadcasted_iota(jnp.int32, shape, 1)
        key_pos = first_row + (i * BLOCK - HALF) + key
        allowed = (key >= query) & (key < query + WINDOW) & (key_pos >= 0) & (key_pos < length)
        bias[i] = jnp.where(allowed, 0.0, -1e30)


def forward(hh, i, q_ref, cols, kx, vx, bias, prob, att, length, first_row):
    hc = slice(hh * HEAD_DIM, (hh + 1) * HEAD_DIM)
    rows = slice(i * BLOCK, (i + 1) * BLOCK)
    win = slice(i * BLOCK, i * BLOCK + BLOCK + 2 * HALF)
    qh = q_ref[rows, cols][:, hc]
    t = mm(kx[win, hc], qh, NT) * (INV_ROOT * LOG2E) + bias[i]
    top = jnp.max(t, axis=0, keepdims=True)
    e = jnp.exp2(t - top)
    total = jnp.maximum(jnp.sum(e, axis=0, keepdims=True), 1.0)
    pos = first_row + i * BLOCK + lax.broadcasted_iota(jnp.int32, (1, BLOCK), 1)
    p = e * jnp.where(pos < length, 1.0 / total, 0.0)
    prob[hh, i] = p
    att[hc, rows] = mm(vx[win, hc], p.astype(jnp.bfloat16), TN).astype(jnp.bfloat16)


def backward(hh, i, q_ref, cols, kx, vx, g, prob, gq_ref, gk_acc, gv_acc):
    hc = slice(hh * HEAD_DIM, (hh + 1) * HEAD_DIM)
    rows = slice(i * BLOCK, (i + 1) * BLOCK)
    span = BLOCK + 2 * HALF
    win = slice(i * BLOCK, i * BLOCK + span)
    qh = q_ref[rows, cols][:, hc]
    gh = g[rows, hc]
    kw = kx[win, hc]
    p = prob[hh, i]
    dp = mm(vx[win, hc], gh, NT)
    delta = jnp.sum(p * dp, axis=0, keepdims=True)
    gs = (p * (dp - delta)).astype(jnp.bfloat16)
    gq = (mm(kw, gs, TN) * INV_ROOT).T
    gq_ref[rows, pl.ds(cols.start + hh * HEAD_DIM, HEAD_DIM)] = gq.astype(jnp.bfloat16)
    gk = mm(gs, qh, NN) * INV_ROOT
    gv = mm(p.astype(jnp.bfloat16), gh, NN)
    for acc, new in ((gk_acc, gk), (gv_acc, gv)):
        if i == 0:
            acc[win, hc] = new
        else:
            old = slice(i * BLOCK, i * BLOCK + 2 * HALF)
            acc[old, hc] += new[: 2 * HALF]
            acc[i * BLOCK + 2 * HALF : i * BLOCK + span, hc] = new[2 * HALF :]


def ring_add(index, by, count):
    return lax.rem(index + by, count)


def kernel(
    count, seq, len_ref, q_ref, k_ref, v_ref, go_ref, w_ref,
    gq_ref, gk_ref, gv_ref, wg_ref,
    bias, got, kx, vx, g, prob, att, gk_acc, gv_acc,
    w_all, halo, rim, own, part, fin, piece, piece_in,
    keeps, sends, recvs,
    w_send, w_recv, w_pass, halo_send, halo_recv, rim_send, rim_recv,
    red_send, red_recv, piece_send, piece_recv,
):
    tok, width = q_ref.shape
    groups = width // COLS
    chips = count // 2
    stages = len(keeps)
    depth = w_ref.shape[0]
    dp, z = lax.axis_index("dp"), lax.axis_index("seq")
    chip, core = lax.div(dp, 2), lax.rem(dp, 2)
    sibling = dp + 1 - 2 * core
    first_row = z * tok
    length = len_ref[0]
    rows_out = wg_ref.shape[0]
    split_seq = rows_out != depth

    def copy(source, target, send_sem, recv_sem, to_dp, to_z):
        return pltpu.make_async_remote_copy(
            src_ref=source, dst_ref=target, send_sem=send_sem, recv_sem=recv_sem,
            device_id=(to_dp, to_z), device_id_type=pl.DeviceIdType.MESH,
        )

    def columns(n):
        return pl.ds(pl.multiple_of(n * COLS, COLS), COLS)

    def same_core(d):
        return 2 * ring_add(chip, d, chips) + core

    def weight_copy(n, d):
        to = sibling if d == 0 else same_core(d)
        return copy(w_ref.at[:, columns(n)], w_all.at[n, dp], w_send.at[n, d], w_recv.at[n, dp], to, z)

    def weight_from(n, block, to):
        return copy(w_all.at[n, block], w_all.at[n, block], w_pass.at[n, 0], w_recv.at[n, block], to, z)

    def weight_pass(n, d):
        block = same_core(d)
        return copy(
            w_all.at[n, block], w_all.at[n, block], w_pass.at[n, d], w_recv.at[n, block], sibling, z
        )

    def halo_copy(n, side, s):
        ref = (k_ref, v_ref)[s]
        start = tok - HALF if side == 0 else 0
        return copy(
            ref.at[pl.ds(start, HALF), columns(n)], halo.at[side, s, n],
            halo_send.at[side, s, n], halo_recv.at[side, s, n], dp, z + 1 - 2 * side,
        )

    def rim_copy(n, side, s):
        return copy(
            halo.at[side, s, n], rim.at[1 - side, s, n],
            rim_send.at[side, s, n], rim_recv.at[1 - side, s, n], dp, z - 1 + 2 * side,
        )

    def reduce_copy(s, n):
        bit = lax.rem(lax.div(dp, 2**s), 2)
        return copy(
            sends[s].at[n], recvs[s].at[n], red_send.at[s, n], red_recv.at[s, n],
            dp + (1 - 2 * bit) * 2**s, z,
        )

    def piece_copy(n, d):
        to = ring_add(z, d, seq)
        rows = pl.ds(pl.multiple_of(to * rows_out, 16), rows_out)
        return copy(
            piece.at[n, rows], piece_in.at[n, z], piece_send.at[n, d], piece_recv.at[n, z], dp, to
        )

    def piece_from(n, d):
        block = ring_add(z, d, seq)
        rows = pl.ds(pl.multiple_of(block * rows_out, 16), rows_out)
        return copy(
            piece.at[n, rows], piece_in.at[n, block], piece_send.at[n, d], piece_recv.at[n, block],
            dp, block,
        )

    has_before, has_after = z > 0, z < seq - 1
    exists = (has_before, has_after)

    barrier = pltpu.get_barrier_semaphore()
    peers = [(sibling, z)]
    peers += [(same_core(d), z) for d in range(1, chips)]
    peers += [(dp, ring_add(z, d, seq)) for d in range(1, seq)]
    for peer in peers:
        pl.semaphore_signal(barrier, inc=1, device_id=peer, device_id_type=pl.DeviceIdType.MESH)
    pl.semaphore_wait(barrier, len(peers))

    def begin(n):
        for d in range(chips):
            weight_copy(n, d).start()
        for side in range(2):
            @pl.when(exists[1 - side])
            def _():
                for s in range(2):
                    halo_copy(n, side, s).start()
        w_all[n, dp] = w_ref[:, columns(n)]

    begin(0)
    for side in range(2):
        @pl.when(jnp.logical_not(exists[side]))
        def _():
            halo[side] = jnp.zeros(halo.shape[1:], halo.dtype)

    fill_bias(bias, length, first_row)
    got[...] = go_ref[...].T
    begin(1)

    def pass_weight(n):
        for d in range(1, chips):
            weight_from(n, same_core(d), sibling).wait_recv()
            weight_pass(n, d).start()

    def reduce_stage(s, n):
        slot = lax.rem(n, 2)
        if s > 0:
            reduce_copy(s - 1, n).wait_recv()

        def held(i):
            if s == 0:
                return part[i]
            return keeps[s - 1][slot, i] + recvs[s - 1][n, i].astype(jnp.float32)

        if s == stages:
            fin[n] = held(0)
            if split_seq:
                piece[n] = fin[n].astype(jnp.bfloat16)
                for d in range(1, seq):
                    piece_copy(n, d).start()
            return
        bit = lax.rem(lax.div(dp, 2**s), 2)
        for i in range(keeps[s].shape[1]):
            sends[s][n, i] = held(2 * i + 1 - bit).astype(jnp.bfloat16)
            keeps[s][slot, i] = held(2 * i + bit)
        reduce_copy(s, n).start()

    def stage_if(s, n):
        if s <= stages:
            @pl.when((n >= 0) & (n < groups))
            def _():
                reduce_stage(s, n)

    def even_stages(n):
        for s in range(stages - stages % 2, 1, -2):
            stage_if(s, n - s // 2)

    def odd_stages(n):
        for s in range(stages - 1 + stages % 2, 2, -2):
            stage_if(s, n - s // 2)

    def add_rims(n):
        cols = columns(n)
        for side in range(2):
            rows = pl.ds(0 if side == 0 else tok - HALF, HALF)

            @pl.when(exists[side])
            def _():
                for s in range(2):
                    rim_copy(n, 1 - side, s).wait_recv()
                    own[s, n, rows] += rim[side, s, n].astype(jnp.float32)

        gk_ref[:, cols] = own[0, n].astype(jnp.bfloat16)
        gv_ref[:, cols] = own[1, n].astype(jnp.bfloat16)

    pass_weight(0)

    def step(n, carry):
        cols = columns(n)
        for side in range(2):
            @pl.when(exists[side])
            def _():
                for s in range(2):
                    halo_copy(n, side, s).wait_recv()

        @pl.when(n + 2 < groups)
        def _():
            begin(n + 2)

        for s, (x, ref) in enumerate(((kx, k_ref), (vx, v_ref))):
            x[:HALF] = halo[0, s, n]
            x[HALF : HALF + tok] = ref[:, cols]
            x[HALF + tok :] = halo[1, s, n]
        chains = [(hh, i) for hh in range(GROUP) for i in range(tok // BLOCK)]
        for hh, i in chains:
            forward(hh, i, q_ref, cols, kx, vx, bias, prob, att, length, first_row)
        part[...] = mm(got[...], att[...], NT).reshape(part.shape)
        reduce_stage(0, n)
        even_stages(n)
        for d in range(chips):
            weight_from(n, same_core(d) + 1 - 2 * core, sibling).wait_recv()
        weight = w_all[n].reshape(count * depth, COLS)
        g[...] = mm(go_ref[...], weight, NN).astype(jnp.bfloat16)
        for c, (hh, i) in enumerate(chains):
            backward(hh, i, q_ref, cols, kx, vx, g, prob, gq_ref, gk_acc, gv_acc)
            if c == 0:
                reduce_stage(1, n)
            if c == len(chains) // 2:
                odd_stages(n)
        for s, acc in enumerate((gk_acc, gv_acc)):
            halo[0, s, n] = acc[:HALF].astype(jnp.bfloat16)
            halo[1, s, n] = acc[HALF + tok :].astype(jnp.bfloat16)
        for side in range(2):
            @pl.when(exists[side])
            def _():
                for s in range(2):
                    rim_copy(n, side, s).start()

        for s, acc in enumerate((gk_acc, gv_acc)):
            own[s, n] = acc[HALF : HALF + tok]

        @pl.when(n + 1 < groups)
        def _():
            pass_weight(n + 1)

        @pl.when(n >= 2)
        def _():
            add_rims(n - 2)

        return carry

    lax.fori_loop(0, groups, step, 0)

    for late in range((stages + 1) // 2):
        even_stages(groups + late)
        odd_stages(groups + late)

    def finish(n, carry):
        cols = columns(n)
        @pl.when(n >= groups - 2)
        def _():
            add_rims(n)

        if split_seq:
            total = fin[n, pl.ds(pl.multiple_of(z * rows_out, 16), rows_out)]
            for d in range(1, seq):
                piece_from(n, d).wait_recv()
                total += piece_in[n, ring_add(z, d, seq)].astype(jnp.float32)
            wg_ref[:, cols] = total
        else:
            wg_ref[:, cols] = fin[n]
        for d in range(chips):
            weight_copy(n, d).wait_send()
        for d in range(1, chips):
            weight_pass(n, d).wait_send()
        for side in range(2):
            @pl.when(exists[1 - side])
            def _():
                for s in range(2):
                    halo_copy(n, side, s).wait_send()

            @pl.when(exists[side])
            def _():
                for s in range(2):
                    rim_copy(n, side, s).wait_send()
        for s in range(stages):
            reduce_copy(s, n).wait_send()
        if split_seq:
            for d in range(1, seq):
                piece_copy(n, d).wait_send()
        return carry

    lax.fori_loop(0, groups, finish, 0)


def copy_kernel(*refs):
    half = len(refs) // 2
    for source, target in zip(refs[:half], refs[half:]):
        target[...] = source[...]


def handed_on(*arrays):
    steps = 4 if all(x.shape[0] % 64 == 0 for x in arrays[:-1]) else 1

    def spec(x):
        rows = x.shape[0] // steps if x.shape[0] % (steps * 8) == 0 else x.shape[0]
        whole = rows == x.shape[0]
        return pl.BlockSpec((rows, x.shape[1]), (lambda n: (0, 0)) if whole else (lambda n: (n, 0)))

    specs = [spec(x) for x in arrays]
    return pl.pallas_call(
        copy_kernel,
        grid=(steps,),
        out_shape=[jax.ShapeDtypeStruct(x.shape, x.dtype) for x in arrays],
        in_specs=specs,
        out_specs=specs,
        compiler_params=pltpu.CompilerParams(vmem_limit_bytes=32 * 1024 * 1024),
    )(*arrays)


def shards(queries, keys, values, grad_out, out_weight, lengths):
    tok, width = queries.shape
    depth = out_weight.shape[0]
    count, seq = lax.axis_size("dp"), lax.axis_size("seq")
    stages = count.bit_length() - 1
    groups = width // COLS
    wide = tok + 2 * HALF
    split_seq = seq > 1 and (depth // seq) % 16 == 0
    rows_out = depth // seq if split_seq else depth
    vmem = pl.BlockSpec(memory_space=pltpu.VMEM)
    smem = pl.BlockSpec(memory_space=pltpu.SMEM)
    bf, f32 = jnp.bfloat16, jnp.float32
    dma = pltpu.SemaphoreType.DMA
    halves = [count >> (s + 1) for s in range(stages)]
    grad_query, grad_key, grad_value, weight_grad = pl.pallas_call(
        functools.partial(kernel, count, seq),
        out_shape=(
            jax.ShapeDtypeStruct((tok, width), bf),
            jax.ShapeDtypeStruct((tok, width), bf),
            jax.ShapeDtypeStruct((tok, width), bf),
            jax.ShapeDtypeStruct((rows_out, width), f32),
        ),
        in_specs=[smem] + [vmem] * 5,
        out_specs=(vmem,) * 4,
        scratch_shapes=[
            pltpu.VMEM((tok // BLOCK, BLOCK + 2 * HALF, BLOCK), f32),
            pltpu.VMEM((width, tok), bf),
            pltpu.VMEM((wide, COLS), bf),
            pltpu.VMEM((wide, COLS), bf),
            pltpu.VMEM((tok, COLS), bf),
            pltpu.VMEM((GROUP, tok // BLOCK, BLOCK + 2 * HALF, BLOCK), f32),
            pltpu.VMEM((COLS, tok), bf),
            pltpu.VMEM((wide, COLS), f32),
            pltpu.VMEM((wide, COLS), f32),
            pltpu.VMEM((groups, count, depth, COLS), bf),
            pltpu.VMEM((2, 2, groups, HALF, COLS), bf),
            pltpu.VMEM((2, 2, groups, HALF, COLS), bf),
            pltpu.VMEM((2, groups, tok, COLS), f32),
            pltpu.VMEM((count, depth, COLS), f32),
            pltpu.VMEM((groups, depth, COLS), f32),
            pltpu.VMEM((groups, depth, COLS), bf),
            pltpu.VMEM((groups, seq, depth // seq if split_seq else 16, COLS), bf),
            [pltpu.VMEM((2, h, depth, COLS), f32) for h in halves],
            [pltpu.VMEM((groups, h, depth, COLS), bf) for h in halves],
            [pltpu.VMEM((groups, h, depth, COLS), bf) for h in halves],
            dma((groups, count // 2)),
            dma((groups, count)),
            dma((groups, count // 2)),
            dma((2, 2, groups)),
            dma((2, 2, groups)),
            dma((2, 2, groups)),
            dma((2, 2, groups)),
            dma((stages, groups)),
            dma((stages, groups)),
            dma((groups, seq)),
            dma((groups, seq)),
        ],
        compiler_params=pltpu.CompilerParams(
            vmem_limit_bytes=62 * 1024 * 1024, collective_id=0, has_side_effects=True
        ),
        cost_estimate=pl.CostEstimate(
            flops=20_000_000_000, bytes_accessed=12_000_000, transcendentals=5_000_000
        ),
    )(lengths, queries, keys, values, grad_out, out_weight)
    if not split_seq:
        weight_grad = lax.psum_scatter(weight_grad, "seq", scatter_dimension=0, tiled=True)
    return handed_on(grad_query, grad_key, grad_value, weight_grad)


def solution(mesh):
    rows = P(("dp", "seq"), None)
    in_specs = (rows, rows, rows, rows, P("dp", None), P("dp"))
    return jax.shard_map(
        shards, mesh=mesh, in_specs=in_specs, out_specs=(rows,) * 4, check_vma=False
    )
```

```python
import functools

import jax
import jax.numpy as jnp
from jax import lax
from jax.experimental import pallas as pl
from jax.experimental.pallas import tpu as pltpu
from jax.sharding import PartitionSpec as P

HEADS = 12
HEAD_DIM = 128
WINDOW = 512
HALF = WINDOW // 2
GROUP = 2
COLS = GROUP * HEAD_DIM
BLOCK = HALF
INV_ROOT = HEAD_DIM ** (-0.5)
LOG2E = 1.4426950408889634
NT = (((1,), (1,)), ((), ()))
NN = (((1,), (0,)), ((), ()))
TN = (((0,), (0,)), ((), ()))


def mm(a, b, dims):
    return lax.dot_general(a, b, dims, preferred_element_type=jnp.float32)


def fill_bias(bias, length, first_row):
    for i in range(bias.shape[0]):
        shape = (BLOCK + 2 * HALF, BLOCK)
        key = lax.broadcasted_iota(jnp.int32, shape, 0)
        query = lax.broadcasted_iota(jnp.int32, shape, 1)
        key_pos = first_row + (i * BLOCK - HALF) + key
        allowed = (key >= query) & (key < query + WINDOW) & (key_pos >= 0) & (key_pos < length)
        bias[i] = jnp.where(allowed, 0.0, -1e30)


def forward(hh, i, q_ref, cols, kx, vx, bias, prob, att, length, first_row):
    hc = slice(hh * HEAD_DIM, (hh + 1) * HEAD_DIM)
    rows = slice(i * BLOCK, (i + 1) * BLOCK)
    win = slice(i * BLOCK, i * BLOCK + BLOCK + 2 * HALF)
    qh = q_ref[rows, cols][:, hc]
    t = mm(kx[win, hc], qh, NT) * (INV_ROOT * LOG2E) + bias[i]
    top = jnp.max(t, axis=0, keepdims=True)
    e = jnp.exp2(t - top)
    total = jnp.maximum(jnp.sum(e, axis=0, keepdims=True), 1.0)
    pos = first_row + i * BLOCK + lax.broadcasted_iota(jnp.int32, (1, BLOCK), 1)
    p = e * jnp.where(pos < length, 1.0 / total, 0.0)
    prob[hh, i] = p
    att[hc, rows] = mm(vx[win, hc], p.astype(jnp.bfloat16), TN).astype(jnp.bfloat16)


def backward(hh, i, q_ref, cols, kx, vx, g, prob, staged, n, gk_acc, gv_acc):
    hc = slice(hh * HEAD_DIM, (hh + 1) * HEAD_DIM)
    rows = slice(i * BLOCK, (i + 1) * BLOCK)
    span = BLOCK + 2 * HALF
    win = slice(i * BLOCK, i * BLOCK + span)
    qh = q_ref[rows, cols][:, hc]
    gh = g[rows, hc]
    kw = kx[win, hc]
    p = prob[hh, i]
    dp = mm(vx[win, hc], gh, NT)
    delta = jnp.sum(p * dp, axis=0, keepdims=True)
    gs = (p * (dp - delta)).astype(jnp.bfloat16)
    gq = (mm(kw, gs, TN) * INV_ROOT).T
    staged[0, n, rows, hc] = gq.astype(jnp.bfloat16)
    gk = mm(gs, qh, NN) * INV_ROOT
    gv = mm(p.astype(jnp.bfloat16), gh, NN)
    for acc, new in ((gk_acc, gk), (gv_acc, gv)):
        if i == 0:
            acc[win, hc] = new
        else:
            old = slice(i * BLOCK, i * BLOCK + 2 * HALF)
            acc[old, hc] += new[: 2 * HALF]
            acc[i * BLOCK + 2 * HALF : i * BLOCK + span, hc] = new[2 * HALF :]


def ring_add(index, by, count):
    return lax.rem(index + by, count)


def kernel(
    count, seq, len_ref, q_hbm, k_hbm, v_hbm, go_hbm, w_ref,
    gq_hbm, gk_hbm, gv_hbm, wg_ref,
    q_ref, k_ref, v_ref, go_ref, load_sem, weight_sem, staged, store_sem,
    bias, got, kx, vx, g, prob, att, gk_acc, gv_acc,
    w_all, halo, rim, own, part, fin, piece, piece_in,
    keeps, sends, recvs,
    w_send, w_recv, w_pass, halo_send, halo_recv, rim_send, rim_recv,
    red_send, red_recv, piece_send, piece_recv,
):
    tok, width = q_hbm.shape
    groups = width // COLS
    chips = count // 2
    stages = len(keeps)
    depth = w_ref.shape[0]
    dp, z = lax.axis_index("dp"), lax.axis_index("seq")
    chip, core = lax.div(dp, 2), lax.rem(dp, 2)
    sibling = dp + 1 - 2 * core
    first_row = z * tok
    length = len_ref[0]
    rows_out = wg_ref.shape[0]
    split_seq = rows_out != depth

    def copy(source, target, send_sem, recv_sem, to_dp, to_z):
        return pltpu.make_async_remote_copy(
            src_ref=source, dst_ref=target, send_sem=send_sem, recv_sem=recv_sem,
            device_id=(to_dp, to_z), device_id_type=pl.DeviceIdType.MESH,
        )

    def columns(n):
        return pl.ds(pl.multiple_of(n * COLS, COLS), COLS)

    def same_core(d):
        return 2 * ring_add(chip, d, chips) + core

    def weight_copy(n, d):
        to = sibling if d == 0 else same_core(d)
        return copy(w_ref.at[:, columns(n)], w_all.at[n, dp], w_send.at[n, d], w_recv.at[n, dp], to, z)

    def weight_from(n, block, to):
        return copy(w_all.at[n, block], w_all.at[n, block], w_pass.at[n, 0], w_recv.at[n, block], to, z)

    def weight_pass(n, d):
        block = same_core(d)
        return copy(
            w_all.at[n, block], w_all.at[n, block], w_pass.at[n, d], w_recv.at[n, block], sibling, z
        )

    def halo_copy(n, side, s):
        ref = (k_hbm, v_hbm)[s]
        start = tok - HALF if side == 0 else 0
        return copy(
            ref.at[pl.ds(start, HALF), columns(n)], halo.at[side, s, n],
            halo_send.at[side, s, n], halo_recv.at[side, s, n], dp, z + 1 - 2 * side,
        )

    def rim_copy(n, side, s):
        return copy(
            halo.at[side, s, n], rim.at[1 - side, s, n],
            rim_send.at[side, s, n], rim_recv.at[1 - side, s, n], dp, z - 1 + 2 * side,
        )

    def reduce_copy(s, n):
        bit = lax.rem(lax.div(dp, 2**s), 2)
        return copy(
            sends[s].at[n], recvs[s].at[n], red_send.at[s, n], red_recv.at[s, n],
            dp + (1 - 2 * bit) * 2**s, z,
        )

    def piece_copy(n, d):
        to = ring_add(z, d, seq)
        rows = pl.ds(pl.multiple_of(to * rows_out, 16), rows_out)
        return copy(
            piece.at[n, rows], piece_in.at[n, z], piece_send.at[n, d], piece_recv.at[n, z], dp, to
        )

    def piece_from(n, d):
        block = ring_add(z, d, seq)
        rows = pl.ds(pl.multiple_of(block * rows_out, 16), rows_out)
        return copy(
            piece.at[n, rows], piece_in.at[n, block], piece_send.at[n, d], piece_recv.at[n, block],
            dp, block,
        )

    def load(i):
        source = (go_hbm, q_hbm, k_hbm, v_hbm)[i]
        return pltpu.make_async_copy(source, (go_ref, q_ref, k_ref, v_ref)[i], load_sem.at[i])

    def weight_load(n):
        return pltpu.make_async_copy(w_ref.at[:, columns(n)], w_all.at[n, dp], weight_sem.at[n])

    def store(n, i):
        target = (gq_hbm, gk_hbm, gv_hbm)[i]
        return pltpu.make_async_copy(staged.at[i, n], target.at[:, columns(n)], store_sem.at[i, n])

    has_before, has_after = z > 0, z < seq - 1
    exists = (has_before, has_after)

    for i in range(4):
        load(i).start()
    barrier = pltpu.get_barrier_semaphore()
    peers = [(sibling, z)]
    peers += [(same_core(d), z) for d in range(1, chips)]
    peers += [(dp, ring_add(z, d, seq)) for d in range(1, seq)]
    for peer in peers:
        pl.semaphore_signal(barrier, inc=1, device_id=peer, device_id_type=pl.DeviceIdType.MESH)
    pl.semaphore_wait(barrier, len(peers))

    def begin(n):
        for d in range(chips):
            weight_copy(n, d).start()
        for side in range(2):
            @pl.when(exists[1 - side])
            def _():
                for s in range(2):
                    halo_copy(n, side, s).start()
        weight_load(n).start()

    begin(0)
    for side in range(2):
        @pl.when(jnp.logical_not(exists[side]))
        def _():
            halo[side] = jnp.zeros(halo.shape[1:], halo.dtype)

    fill_bias(bias, length, first_row)
    begin(1)
    load(0).wait()
    got[...] = go_ref[...].T
    begin(2)
    for i in range(1, 4):
        load(i).wait()

    def pass_weight(n):
        for d in range(1, chips):
            weight_from(n, same_core(d), sibling).wait_recv()
            weight_pass(n, d).start()

    def reduce_stage(s, n):
        slot = lax.rem(n, 2)
        if s > 0:
            reduce_copy(s - 1, n).wait_recv()

        def held(i):
            if s == 0:
                return part[i]
            return keeps[s - 1][slot, i] + recvs[s - 1][n, i].astype(jnp.float32)

        if s == stages:
            fin[n] = held(0)
            if split_seq:
                piece[n] = fin[n].astype(jnp.bfloat16)
                for d in range(1, seq):
                    piece_copy(n, d).start()
            return
        bit = lax.rem(lax.div(dp, 2**s), 2)
        for i in range(keeps[s].shape[1]):
            sends[s][n, i] = held(2 * i + 1 - bit).astype(jnp.bfloat16)
            keeps[s][slot, i] = held(2 * i + bit)
        reduce_copy(s, n).start()

    def stage_if(s, n):
        if s <= stages:
            @pl.when((n >= 0) & (n < groups))
            def _():
                reduce_stage(s, n)

    def even_stages(n):
        for s in range(stages - stages % 2, 1, -2):
            stage_if(s, n - s // 2)

    def odd_stages(n):
        for s in range(stages - 1 + stages % 2, 2, -2):
            stage_if(s, n - s // 2)

    def add_rims(n):
        for side in range(2):
            rows = pl.ds(0 if side == 0 else tok - HALF, HALF)

            @pl.when(exists[side])
            def _():
                for s in range(2):
                    rim_copy(n, 1 - side, s).wait_recv()
                    own[s, n, rows] += rim[side, s, n].astype(jnp.float32)

        for s in range(2):
            staged[1 + s, n] = own[s, n].astype(jnp.bfloat16)
            store(n, 1 + s).start()

    pass_weight(0)

    def step(n, carry):
        cols = columns(n)
        for side in range(2):
            @pl.when(exists[side])
            def _():
                for s in range(2):
                    halo_copy(n, side, s).wait_recv()

        @pl.when(n + 3 < groups)
        def _():
            begin(n + 3)

        for s, (x, ref) in enumerate(((kx, k_ref), (vx, v_ref))):
            x[:HALF] = halo[0, s, n]
            x[HALF : HALF + tok] = ref[:, cols]
            x[HALF + tok :] = halo[1, s, n]
        chains = [(hh, i) for hh in range(GROUP) for i in range(tok // BLOCK)]
        for hh, i in chains:
            forward(hh, i, q_ref, cols, kx, vx, bias, prob, att, length, first_row)
        part[...] = mm(got[...], att[...], NT).reshape(part.shape)
        reduce_stage(0, n)
        even_stages(n)
        for d in range(chips):
            weight_from(n, same_core(d) + 1 - 2 * core, sibling).wait_recv()
        weight_load(n).wait()
        weight = w_all[n].reshape(count * depth, COLS)
        g[...] = mm(go_ref[...], weight, NN).astype(jnp.bfloat16)
        for c, (hh, i) in enumerate(chains):
            backward(hh, i, q_ref, cols, kx, vx, g, prob, staged, n, gk_acc, gv_acc)
            if c == 0:
                reduce_stage(1, n)
            if c == len(chains) // 2:
                odd_stages(n)
        for s, acc in enumerate((gk_acc, gv_acc)):
            halo[0, s, n] = acc[:HALF].astype(jnp.bfloat16)
            halo[1, s, n] = acc[HALF + tok :].astype(jnp.bfloat16)
        for side in range(2):
            @pl.when(exists[side])
            def _():
                for s in range(2):
                    rim_copy(n, side, s).start()

        store(n, 0).start()
        for s, acc in enumerate((gk_acc, gv_acc)):
            own[s, n] = acc[HALF : HALF + tok]

        @pl.when(n + 1 < groups)
        def _():
            pass_weight(n + 1)

        @pl.when(n >= 2)
        def _():
            add_rims(n - 2)

        return carry

    lax.fori_loop(0, groups, step, 0)

    for late in range((stages + 1) // 2):
        even_stages(groups + late)
        odd_stages(groups + late)

    def finish(n, carry):
        cols = columns(n)
        @pl.when(n >= groups - 2)
        def _():
            add_rims(n)

        if split_seq:
            total = fin[n, pl.ds(pl.multiple_of(z * rows_out, 16), rows_out)]
            for d in range(1, seq):
                piece_from(n, d).wait_recv()
                total += piece_in[n, ring_add(z, d, seq)].astype(jnp.float32)
            wg_ref[:, cols] = total
        else:
            wg_ref[:, cols] = fin[n]
        for i in range(3):
            store(n, i).wait()
        for d in range(chips):
            weight_copy(n, d).wait_send()
        for d in range(1, chips):
            weight_pass(n, d).wait_send()
        for side in range(2):
            @pl.when(exists[1 - side])
            def _():
                for s in range(2):
                    halo_copy(n, side, s).wait_send()

            @pl.when(exists[side])
            def _():
                for s in range(2):
                    rim_copy(n, side, s).wait_send()
        for s in range(stages):
            reduce_copy(s, n).wait_send()
        if split_seq:
            for d in range(1, seq):
                piece_copy(n, d).wait_send()
        return carry

    lax.fori_loop(0, groups, finish, 0)


def copy_kernel(*refs):
    half = len(refs) // 2
    for source, target in zip(refs[:half], refs[half:]):
        target[...] = source[...]


def handed_on(*arrays):
    steps = 4 if all(x.shape[0] % 64 == 0 for x in arrays[:-1]) else 1

    def spec(x):
        rows = x.shape[0] // steps if x.shape[0] % (steps * 8) == 0 else x.shape[0]
        whole = rows == x.shape[0]
        return pl.BlockSpec((rows, x.shape[1]), (lambda n: (0, 0)) if whole else (lambda n: (n, 0)))

    specs = [spec(x) for x in arrays]
    return pl.pallas_call(
        copy_kernel,
        grid=(steps,),
        out_shape=[jax.ShapeDtypeStruct(x.shape, x.dtype) for x in arrays],
        in_specs=specs,
        out_specs=specs,
        compiler_params=pltpu.CompilerParams(vmem_limit_bytes=62 * 1024 * 1024),
    )(*arrays)


def shards(queries, keys, values, grad_out, out_weight, lengths):
    tok, width = queries.shape
    depth = out_weight.shape[0]
    count, seq = lax.axis_size("dp"), lax.axis_size("seq")
    stages = count.bit_length() - 1
    groups = width // COLS
    wide = tok + 2 * HALF
    split_seq = seq > 1 and (depth // seq) % 16 == 0
    rows_out = depth // seq if split_seq else depth
    vmem = pl.BlockSpec(memory_space=pltpu.VMEM)
    hbm = pl.BlockSpec(memory_space=pl.ANY)
    smem = pl.BlockSpec(memory_space=pltpu.SMEM)
    bf, f32 = jnp.bfloat16, jnp.float32
    dma = pltpu.SemaphoreType.DMA
    halves = [count >> (s + 1) for s in range(stages)]
    grad_query, grad_key, grad_value, weight_grad = pl.pallas_call(
        functools.partial(kernel, count, seq),
        out_shape=(
            jax.ShapeDtypeStruct((tok, width), bf),
            jax.ShapeDtypeStruct((tok, width), bf),
            jax.ShapeDtypeStruct((tok, width), bf),
            jax.ShapeDtypeStruct((rows_out, width), f32),
        ),
        in_specs=[smem] + [hbm] * 5,
        out_specs=(hbm, hbm, hbm, vmem),
        scratch_shapes=[
            pltpu.VMEM((tok, width), bf),
            pltpu.VMEM((tok, width), bf),
            pltpu.VMEM((tok, width), bf),
            pltpu.VMEM((tok, width), bf),
            dma((4,)),
            dma((groups,)),
            pltpu.VMEM((3, groups, tok, COLS), bf),
            dma((3, groups)),
            pltpu.VMEM((tok // BLOCK, BLOCK + 2 * HALF, BLOCK), f32),
            pltpu.VMEM((width, tok), bf),
            pltpu.VMEM((wide, COLS), bf),
            pltpu.VMEM((wide, COLS), bf),
            pltpu.VMEM((tok, COLS), bf),
            pltpu.VMEM((GROUP, tok // BLOCK, BLOCK + 2 * HALF, BLOCK), f32),
            pltpu.VMEM((COLS, tok), bf),
            pltpu.VMEM((wide, COLS), f32),
            pltpu.VMEM((wide, COLS), f32),
            pltpu.VMEM((groups, count, depth, COLS), bf),
            pltpu.VMEM((2, 2, groups, HALF, COLS), bf),
            pltpu.VMEM((2, 2, groups, HALF, COLS), bf),
            pltpu.VMEM((2, groups, tok, COLS), f32),
            pltpu.VMEM((count, depth, COLS), f32),
            pltpu.VMEM((groups, depth, COLS), f32),
            pltpu.VMEM((groups, depth, COLS), bf),
            pltpu.VMEM((groups, seq, depth // seq if split_seq else 16, COLS), bf),
            [pltpu.VMEM((2, h, depth, COLS), f32) for h in halves],
            [pltpu.VMEM((groups, h, depth, COLS), bf) for h in halves],
            [pltpu.VMEM((groups, h, depth, COLS), bf) for h in halves],
            dma((groups, count // 2)),
            dma((groups, count)),
            dma((groups, count // 2)),
            dma((2, 2, groups)),
            dma((2, 2, groups)),
            dma((2, 2, groups)),
            dma((2, 2, groups)),
            dma((stages, groups)),
            dma((stages, groups)),
            dma((groups, seq)),
            dma((groups, seq)),
        ],
        compiler_params=pltpu.CompilerParams(
            vmem_limit_bytes=62 * 1024 * 1024, collective_id=0, has_side_effects=True
        ),
        cost_estimate=pl.CostEstimate(
            flops=20_000_000_000, bytes_accessed=12_000_000, transcendentals=5_000_000
        ),
    )(lengths, queries, keys, values, grad_out, out_weight)
    if not split_seq:
        weight_grad = lax.psum_scatter(weight_grad, "seq", scatter_dimension=0, tiled=True)
    return handed_on(grad_query, grad_key, grad_value, weight_grad)


def solution(mesh):
    rows = P(("dp", "seq"), None)
    in_specs = (rows, rows, rows, rows, P("dp", None), P("dp"))
    return jax.shard_map(
        shards, mesh=mesh, in_specs=in_specs, out_specs=(rows,) * 4, check_vma=False
    )
```

```python
import functools

import jax
import jax.numpy as jnp
from jax import lax
from jax.experimental import pallas as pl
from jax.experimental.pallas import tpu as pltpu
from jax.sharding import PartitionSpec as P

HEADS = 12
HEAD_DIM = 128
WINDOW = 512
HALF = WINDOW // 2
GROUP = 2
COLS = GROUP * HEAD_DIM
BLOCK = HALF
INV_ROOT = HEAD_DIM ** (-0.5)
LOG2E = 1.4426950408889634
NT = (((1,), (1,)), ((), ()))
NN = (((1,), (0,)), ((), ()))
TN = (((0,), (0,)), ((), ()))


def mm(a, b, dims):
    return lax.dot_general(a, b, dims, preferred_element_type=jnp.float32)


def fill_bias(bias, length, first_row):
    for i in range(bias.shape[0]):
        shape = (BLOCK + 2 * HALF, BLOCK)
        key = lax.broadcasted_iota(jnp.int32, shape, 0)
        query = lax.broadcasted_iota(jnp.int32, shape, 1)
        key_pos = first_row + (i * BLOCK - HALF) + key
        allowed = (key >= query) & (key < query + WINDOW) & (key_pos >= 0) & (key_pos < length)
        bias[i] = jnp.where(allowed, 0.0, -1e30)


def forward(hh, i, q_ref, cols, kx, vx, bias, prob, att, length, first_row):
    hc = slice(hh * HEAD_DIM, (hh + 1) * HEAD_DIM)
    rows = slice(i * BLOCK, (i + 1) * BLOCK)
    win = slice(i * BLOCK, i * BLOCK + BLOCK + 2 * HALF)
    qh = q_ref[rows, cols][:, hc]
    t = mm(kx[win, hc], qh, NT) * (INV_ROOT * LOG2E) + bias[i]
    top = jnp.max(t, axis=0, keepdims=True)
    e = jnp.exp2(t - top)
    total = jnp.maximum(jnp.sum(e, axis=0, keepdims=True), 1.0)
    pos = first_row + i * BLOCK + lax.broadcasted_iota(jnp.int32, (1, BLOCK), 1)
    p = e * jnp.where(pos < length, 1.0 / total, 0.0)
    prob[hh, i] = p
    att[hc, rows] = mm(vx[win, hc], p.astype(jnp.bfloat16), TN).astype(jnp.bfloat16)


def backward(hh, i, q_ref, cols, kx, vx, g, prob, staged, n, gk_acc, gv_acc):
    hc = slice(hh * HEAD_DIM, (hh + 1) * HEAD_DIM)
    rows = slice(i * BLOCK, (i + 1) * BLOCK)
    span = BLOCK + 2 * HALF
    win = slice(i * BLOCK, i * BLOCK + span)
    qh = q_ref[rows, cols][:, hc]
    gh = g[rows, hc]
    kw = kx[win, hc]
    p = prob[hh, i]
    dp = mm(vx[win, hc], gh, NT)
    delta = jnp.sum(p * dp, axis=0, keepdims=True)
    gs = (p * (dp - delta)).astype(jnp.bfloat16)
    gq = (mm(kw, gs, TN) * INV_ROOT).T
    staged[0, n, rows, hc] = gq.astype(jnp.bfloat16)
    gk = mm(gs, qh, NN) * INV_ROOT
    gv = mm(p.astype(jnp.bfloat16), gh, NN)
    for acc, new in ((gk_acc, gk), (gv_acc, gv)):
        if i == 0:
            acc[win, hc] = new
        else:
            old = slice(i * BLOCK, i * BLOCK + 2 * HALF)
            acc[old, hc] += new[: 2 * HALF]
            acc[i * BLOCK + 2 * HALF : i * BLOCK + span, hc] = new[2 * HALF :]


def ring_add(index, by, count):
    return lax.rem(index + by, count)


def kernel(
    count, seq, len_ref, q_hbm, k_hbm, v_hbm, go_hbm, w_ref,
    gq_hbm, gk_hbm, gv_hbm, wg_ref,
    q_ref, k_ref, v_ref, go_ref, load_sem, weight_sem, staged, store_sem,
    bias, got, kx, vx, g, prob, att, gk_acc, gv_acc,
    w_all, halo, rim, own, part, fin,
    keeps, sends, recvs,
    w_send, w_recv, w_pass, halo_send, halo_recv, rim_send, rim_recv,
    red_send, red_recv,
):
    tok, width = q_hbm.shape
    groups = width // COLS
    chips = count // 2
    stages = len(keeps)
    depth = w_ref.shape[0]
    dp, z = lax.axis_index("dp"), lax.axis_index("seq")
    chip, core = lax.div(dp, 2), lax.rem(dp, 2)
    sibling = dp + 1 - 2 * core
    first_row = z * tok
    length = len_ref[0]
    rows_out = wg_ref.shape[0]
    dp_stages = count.bit_length() - 1

    def copy(source, target, send_sem, recv_sem, to_dp, to_z):
        return pltpu.make_async_remote_copy(
            src_ref=source, dst_ref=target, send_sem=send_sem, recv_sem=recv_sem,
            device_id=(to_dp, to_z), device_id_type=pl.DeviceIdType.MESH,
        )

    def columns(n):
        return pl.ds(pl.multiple_of(n * COLS, COLS), COLS)

    def same_core(d):
        return 2 * ring_add(chip, d, chips) + core

    def weight_copy(n, d):
        to = sibling if d == 0 else same_core(d)
        return copy(w_ref.at[:, columns(n)], w_all.at[n, dp], w_send.at[n, d], w_recv.at[n, dp], to, z)

    def weight_from(n, block, to):
        return copy(w_all.at[n, block], w_all.at[n, block], w_pass.at[n, 0], w_recv.at[n, block], to, z)

    def weight_pass(n, d):
        block = same_core(d)
        return copy(
            w_all.at[n, block], w_all.at[n, block], w_pass.at[n, d], w_recv.at[n, block], sibling, z
        )

    def halo_copy(n, side, s):
        ref = (k_hbm, v_hbm)[s]
        start = tok - HALF if side == 0 else 0
        return copy(
            ref.at[pl.ds(start, HALF), columns(n)], halo.at[side, s, n],
            halo_send.at[side, s, n], halo_recv.at[side, s, n], dp, z + 1 - 2 * side,
        )

    def rim_copy(n, side, s, hh):
        hc = pl.ds(hh * HEAD_DIM, HEAD_DIM)
        return copy(
            halo.at[side, s, n, :, hc], rim.at[1 - side, s, n, :, hc],
            rim_send.at[side, s, n, hh], rim_recv.at[1 - side, s, n, hh], dp, z - 1 + 2 * side,
        )

    def reduce_bit(s):
        return lax.rem(lax.div(dp, 2**s), 2) if s < dp_stages else lax.rem(lax.div(z, 2 ** (s - dp_stages)), 2)

    def reduce_copy(s, n):
        move = 1 - 2 * reduce_bit(s)
        to = (dp + move * 2**s, z) if s < dp_stages else (dp, z + move * 2 ** (s - dp_stages))
        return copy(sends[s].at[n], recvs[s].at[n], red_send.at[s, n], red_recv.at[s, n], *to)

    def load(i):
        source = (go_hbm, q_hbm, k_hbm, v_hbm)[i]
        return pltpu.make_async_copy(source, (go_ref, q_ref, k_ref, v_ref)[i], load_sem.at[i])

    def weight_load(n):
        return pltpu.make_async_copy(w_ref.at[:, columns(n)], w_all.at[n, dp], weight_sem.at[n])

    def store(n, i):
        target = (gq_hbm, gk_hbm, gv_hbm)[i]
        return pltpu.make_async_copy(staged.at[i, n], target.at[:, columns(n)], store_sem.at[i, n])

    has_before, has_after = z > 0, z < seq - 1
    exists = (has_before, has_after)

    for i in range(4):
        load(i).start()
    barrier = pltpu.get_barrier_semaphore()
    peers = [(sibling, z)]
    peers += [(same_core(d), z) for d in range(1, chips)]
    peers += [(dp, ring_add(z, d, seq)) for d in range(1, seq)]
    for peer in peers:
        pl.semaphore_signal(barrier, inc=1, device_id=peer, device_id_type=pl.DeviceIdType.MESH)
    pl.semaphore_wait(barrier, len(peers))

    def begin(n):
        for d in range(chips):
            weight_copy(n, d).start()
        for side in range(2):
            @pl.when(exists[1 - side])
            def _():
                for s in range(2):
                    halo_copy(n, side, s).start()
        weight_load(n).start()

    begin(0)
    for side in range(2):
        @pl.when(jnp.logical_not(exists[side]))
        def _():
            halo[side] = jnp.zeros(halo.shape[1:], halo.dtype)

    fill_bias(bias, length, first_row)
    begin(1)
    load(0).wait()
    got[...] = go_ref[...].T
    begin(2)
    begin(3)
    for i in range(1, 4):
        load(i).wait()

    def pass_weight(n):
        for d in range(1, chips):
            weight_from(n, same_core(d), sibling).wait_recv()
            weight_pass(n, d).start()

    def reduce_stage(s, n):
        slot = lax.rem(n, 2)
        if s > 0:
            reduce_copy(s - 1, n).wait_recv()

        def held(i):
            if s == 0:
                return part[i]
            if s == dp_stages < stages:
                rows = pl.ds(pl.multiple_of(i * rows_out, 16), rows_out)
                return keeps[s - 1][slot, 0, rows] + recvs[s - 1][n, 0, rows].astype(jnp.float32)
            return keeps[s - 1][slot, i] + recvs[s - 1][n, i].astype(jnp.float32)

        if s == stages:
            fin[n] = held(0)
            return
        bit = reduce_bit(s)
        for i in range(keeps[s].shape[1]):
            sends[s][n, i] = held(2 * i + 1 - bit).astype(jnp.bfloat16)
            keeps[s][slot, i] = held(2 * i + bit)
        reduce_copy(s, n).start()

    def stage_if(s, n):
        if s <= stages:
            @pl.when((n >= 0) & (n < groups))
            def _():
                reduce_stage(s, n)

    def even_stages(n):
        for s in range(stages - stages % 2, 1, -2):
            stage_if(s, n - s // 2)

    def odd_stages(n):
        for s in range(stages - 1 + stages % 2, 2, -2):
            stage_if(s, n - s // 2)

    def add_rims(n):
        for side in range(2):
            rows = pl.ds(0 if side == 0 else tok - HALF, HALF)

            @pl.when(exists[side])
            def _():
                for s in range(2):
                    for hh in range(GROUP):
                        rim_copy(n, 1 - side, s, hh).wait_recv()
                    own[s, n, rows] += rim[side, s, n].astype(jnp.float32)

        for s in range(2):
            staged[1 + s, n] = own[s, n].astype(jnp.bfloat16)
            store(n, 1 + s).start()

    chains = [(hh, i) for hh in range(GROUP) for i in range(tok // BLOCK)]

    def ahead(n):
        for side in range(2):
            @pl.when(exists[side])
            def _():
                for s in range(2):
                    halo_copy(n, side, s).wait_recv()

        @pl.when((n >= 1) & (n + 3 < groups))
        def _():
            begin(n + 3)

        cols = columns(n)
        slot = lax.rem(n, 2)
        for s, (x, ref) in enumerate(((kx, k_ref), (vx, v_ref))):
            x[slot, :HALF] = halo[0, s, n]
            x[slot, HALF : HALF + tok] = ref[:, cols]
            x[slot, HALF + tok :] = halo[1, s, n]
        kxs, vxs, probs = kx.at[slot], vx.at[slot], prob.at[slot]
        for hh, i in chains:
            forward(hh, i, q_ref, cols, kxs, vxs, bias, probs, att, length, first_row)
        part[...] = mm(got[...], att[...], NT).reshape(part.shape)
        reduce_stage(0, n)

    ahead(jnp.int32(0))
    pass_weight(0)
    reduce_stage(1, jnp.int32(0))

    def step(n, carry):
        cols = columns(n)
        slot = lax.rem(n, 2)

        @pl.when(n + 1 < groups)
        def _():
            ahead(n + 1)

        even_stages(n + 1)
        for d in range(chips):
            weight_from(n, same_core(d) + 1 - 2 * core, sibling).wait_recv()
        weight_load(n).wait()
        weight = w_all[n].reshape(count * depth, COLS)
        g[...] = mm(go_ref[...], weight, NN).astype(jnp.bfloat16)
        for c, (hh, i) in enumerate(chains):
            backward(
                hh, i, q_ref, cols, kx.at[slot], vx.at[slot], g, prob.at[slot], staged, n, gk_acc, gv_acc
            )
            if c == 0:
                stage_if(1, n + 1)
            if c == len(chains) // 2:
                odd_stages(n + 1)
            if i == tok // BLOCK - 1:
                hc = slice(hh * HEAD_DIM, (hh + 1) * HEAD_DIM)
                for s, acc in enumerate((gk_acc, gv_acc)):
                    halo[0, s, n, :, hc] = acc[:HALF, hc].astype(jnp.bfloat16)
                    halo[1, s, n, :, hc] = acc[HALF + tok :, hc].astype(jnp.bfloat16)
                for side in range(2):
                    @pl.when(exists[side])
                    def _():
                        for s in range(2):
                            rim_copy(n, side, s, hh).start()
        store(n, 0).start()
        for s, acc in enumerate((gk_acc, gv_acc)):
            own[s, n] = acc[HALF : HALF + tok]

        @pl.when(n + 1 < groups)
        def _():
            pass_weight(n + 1)

        @pl.when(n >= 2)
        def _():
            add_rims(n - 2)

        return carry

    lax.fori_loop(0, groups, step, 0)

    for late in range(1, (stages + 1) // 2):
        even_stages(groups + late)
        odd_stages(groups + late)

    def finish(n, carry):
        cols = columns(n)
        @pl.when(n >= groups - 2)
        def _():
            add_rims(n)

        wg_ref[:, cols] = fin[n]
        for i in range(3):
            store(n, i).wait()
        for d in range(chips):
            weight_copy(n, d).wait_send()
        for d in range(1, chips):
            weight_pass(n, d).wait_send()
        for side in range(2):
            @pl.when(exists[1 - side])
            def _():
                for s in range(2):
                    halo_copy(n, side, s).wait_send()

            @pl.when(exists[side])
            def _():
                for s in range(2):
                    for hh in range(GROUP):
                        rim_copy(n, side, s, hh).wait_send()
        for s in range(stages):
            reduce_copy(s, n).wait_send()
        return carry

    lax.fori_loop(0, groups, finish, 0)


def copy_kernel(*refs):
    *refs, read_sem, write_sem = refs
    third = len(refs) // 3
    parts = []
    for i, (source, target, held) in enumerate(zip(refs[:third], refs[third : 2 * third], refs[2 * third :])):
        count = 4 if source.shape[0] % 64 == 0 else 1
        size = source.shape[0] // count
        for j in range(count):
            rows = pl.ds(j * size, size)
            parts.append(
                (
                    pltpu.make_async_copy(source.at[rows], held.at[rows], read_sem.at[i, j]),
                    pltpu.make_async_copy(held.at[rows], target.at[rows], write_sem.at[i, j]),
                )
            )
    for read, write in parts:
        read.start()
    for read, write in parts:
        read.wait()
        write.start()
    for read, write in parts:
        write.wait()


def handed_on(*arrays):
    hbm = pl.BlockSpec(memory_space=pl.ANY)
    return pl.pallas_call(
        copy_kernel,
        out_shape=[jax.ShapeDtypeStruct(x.shape, x.dtype) for x in arrays],
        in_specs=[hbm] * len(arrays),
        out_specs=[hbm] * len(arrays),
        scratch_shapes=[pltpu.VMEM(x.shape, x.dtype) for x in arrays]
        + [pltpu.SemaphoreType.DMA((len(arrays), 4))] * 2,
        compiler_params=pltpu.CompilerParams(vmem_limit_bytes=62 * 1024 * 1024),
    )(*arrays)


def shards(queries, keys, values, grad_out, out_weight, lengths):
    tok, width = queries.shape
    depth = out_weight.shape[0]
    count, seq = lax.axis_size("dp"), lax.axis_size("seq")
    stages = count.bit_length() - 1
    groups = width // COLS
    wide = tok + 2 * HALF
    split_seq = seq > 1 and (depth // seq) % 16 == 0 and seq & (seq - 1) == 0
    rows_out = depth // seq if split_seq else depth
    vmem = pl.BlockSpec(memory_space=pltpu.VMEM)
    hbm = pl.BlockSpec(memory_space=pl.ANY)
    smem = pl.BlockSpec(memory_space=pltpu.SMEM)
    bf, f32 = jnp.bfloat16, jnp.float32
    dma = pltpu.SemaphoreType.DMA
    halves = [(count >> (s + 1), depth) for s in range(stages)]
    if split_seq:
        halves += [(seq >> (s + 1), rows_out) for s in range(seq.bit_length() - 1)]
    grad_query, grad_key, grad_value, weight_grad = pl.pallas_call(
        functools.partial(kernel, count, seq),
        out_shape=(
            jax.ShapeDtypeStruct((tok, width), bf),
            jax.ShapeDtypeStruct((tok, width), bf),
            jax.ShapeDtypeStruct((tok, width), bf),
            jax.ShapeDtypeStruct((rows_out, width), f32),
        ),
        in_specs=[smem] + [hbm] * 5,
        out_specs=(hbm, hbm, hbm, vmem),
        scratch_shapes=[
            pltpu.VMEM((tok, width), bf),
            pltpu.VMEM((tok, width), bf),
            pltpu.VMEM((tok, width), bf),
            pltpu.VMEM((tok, width), bf),
            dma((4,)),
            dma((groups,)),
            pltpu.VMEM((3, groups, tok, COLS), bf),
            dma((3, groups)),
            pltpu.VMEM((tok // BLOCK, BLOCK + 2 * HALF, BLOCK), f32),
            pltpu.VMEM((width, tok), bf),
            pltpu.VMEM((2, wide, COLS), bf),
            pltpu.VMEM((2, wide, COLS), bf),
            pltpu.VMEM((tok, COLS), bf),
            pltpu.VMEM((2, GROUP, tok // BLOCK, BLOCK + 2 * HALF, BLOCK), f32),
            pltpu.VMEM((COLS, tok), bf),
            pltpu.VMEM((wide, COLS), f32),
            pltpu.VMEM((wide, COLS), f32),
            pltpu.VMEM((groups, count, depth, COLS), bf),
            pltpu.VMEM((2, 2, groups, HALF, COLS), bf),
            pltpu.VMEM((2, 2, groups, HALF, COLS), bf),
            pltpu.VMEM((2, groups, tok, COLS), f32),
            pltpu.VMEM((count, depth, COLS), f32),
            pltpu.VMEM((groups, rows_out, COLS), f32),
            [pltpu.VMEM((2,) + h + (COLS,), f32) for h in halves],
            [pltpu.VMEM((groups,) + h + (COLS,), bf) for h in halves],
            [pltpu.VMEM((groups,) + h + (COLS,), bf) for h in halves],
            dma((groups, count // 2)),
            dma((groups, count)),
            dma((groups, count // 2)),
            dma((2, 2, groups)),
            dma((2, 2, groups)),
            dma((2, 2, groups, GROUP)),
            dma((2, 2, groups, GROUP)),
            dma((len(halves), groups)),
            dma((len(halves), groups)),
        ],
        compiler_params=pltpu.CompilerParams(
            vmem_limit_bytes=62 * 1024 * 1024, collective_id=0, has_side_effects=True
        ),
        cost_estimate=pl.CostEstimate(
            flops=20_000_000_000, bytes_accessed=12_000_000, transcendentals=5_000_000
        ),
    )(lengths, queries, keys, values, grad_out, out_weight)
    if not split_seq:
        weight_grad = lax.psum_scatter(weight_grad, "seq", scatter_dimension=0, tiled=True)
    return handed_on(grad_query, grad_key, grad_value, weight_grad)


def solution(mesh):
    rows = P(("dp", "seq"), None)
    in_specs = (rows, rows, rows, rows, P("dp", None), P("dp"))
    return jax.shard_map(
        shards, mesh=mesh, in_specs=in_specs, out_specs=(rows,) * 4, check_vma=False
    )
```

```python
import functools

import jax
import jax.numpy as jnp
from jax import lax
from jax.experimental import pallas as pl
from jax.experimental.pallas import tpu as pltpu
from jax.sharding import PartitionSpec as P

HEADS = 12
HEAD_DIM = 128
WINDOW = 512
HALF = WINDOW // 2
GROUP = 2
COLS = GROUP * HEAD_DIM
BLOCK = HALF
INV_ROOT = HEAD_DIM ** (-0.5)
LOG2E = 1.4426950408889634
NT = (((1,), (1,)), ((), ()))
NN = (((1,), (0,)), ((), ()))
TN = (((0,), (0,)), ((), ()))


def mm(a, b, dims):
    return lax.dot_general(a, b, dims, preferred_element_type=jnp.float32)


def fill_bias(bias, length, first_row):
    for i in range(bias.shape[0]):
        shape = (BLOCK + 2 * HALF, BLOCK)
        key = lax.broadcasted_iota(jnp.int32, shape, 0)
        query = lax.broadcasted_iota(jnp.int32, shape, 1)
        key_pos = first_row + (i * BLOCK - HALF) + key
        allowed = (key >= query) & (key < query + WINDOW) & (key_pos >= 0) & (key_pos < length)
        bias[i] = jnp.where(allowed, 0.0, -1e30)


def forward(hh, i, q_ref, cols, kx, vx, bias, prob, att, length, first_row):
    hc = slice(hh * HEAD_DIM, (hh + 1) * HEAD_DIM)
    rows = slice(i * BLOCK, (i + 1) * BLOCK)
    win = slice(i * BLOCK, i * BLOCK + BLOCK + 2 * HALF)
    qh = q_ref[rows, cols][:, hc]
    t = mm(kx[win, hc], qh, NT) * (INV_ROOT * LOG2E) + bias[i]
    top = jnp.max(t, axis=0, keepdims=True)
    e = jnp.exp2(t - top)
    total = jnp.maximum(jnp.sum(e, axis=0, keepdims=True), 1.0)
    pos = first_row + i * BLOCK + lax.broadcasted_iota(jnp.int32, (1, BLOCK), 1)
    p = e * jnp.where(pos < length, 1.0 / total, 0.0)
    prob[hh, i] = p
    att[hc, rows] = mm(vx[win, hc], p.astype(jnp.bfloat16), TN).astype(jnp.bfloat16)


def backward(hh, i, q_ref, cols, kx, vx, g, prob, staged, n, gk_acc, gv_acc):
    hc = slice(hh * HEAD_DIM, (hh + 1) * HEAD_DIM)
    rows = slice(i * BLOCK, (i + 1) * BLOCK)
    span = BLOCK + 2 * HALF
    win = slice(i * BLOCK, i * BLOCK + span)
    qh = q_ref[rows, cols][:, hc]
    gh = g[rows, hc]
    kw = kx[win, hc]
    p = prob[hh, i]
    dp = mm(vx[win, hc], gh, NT)
    delta = jnp.sum(p * dp, axis=0, keepdims=True)
    gs = (p * (dp - delta)).astype(jnp.bfloat16)
    gq = (mm(kw, gs, TN) * INV_ROOT).T
    staged[0, n, rows, hc] = gq.astype(jnp.bfloat16)
    gk = mm(gs, qh, NN) * INV_ROOT
    gv = mm(p.astype(jnp.bfloat16), gh, NN)
    for acc, new in ((gk_acc, gk), (gv_acc, gv)):
        if i == 0:
            acc[win, hc] = new
        else:
            old = slice(i * BLOCK, i * BLOCK + 2 * HALF)
            acc[old, hc] += new[: 2 * HALF]
            acc[i * BLOCK + 2 * HALF : i * BLOCK + span, hc] = new[2 * HALF :]


def ring_add(index, by, count):
    return lax.rem(index + by, count)


def kernel(
    count, seq, len_ref, q_hbm, k_hbm, v_hbm, go_hbm, w_ref,
    gq_hbm, gk_hbm, gv_hbm, wg_ref,
    q_ref, k_ref, v_ref, go_ref, load_sem, weight_sem, staged, store_sem,
    bias, got, kx, vx, g, prob, att, gk_acc, gv_acc,
    w_all, halo, rim, own, part, fin, piece, piece_in,
    keeps, sends, recvs,
    w_send, w_recv, w_pass, halo_send, halo_recv, rim_send, rim_recv,
    red_send, red_recv, piece_send, piece_recv,
):
    tok, width = q_hbm.shape
    groups = width // COLS
    chips = count // 2
    stages = len(keeps)
    depth = w_ref.shape[0]
    dp, z = lax.axis_index("dp"), lax.axis_index("seq")
    chip, core = lax.div(dp, 2), lax.rem(dp, 2)
    sibling = dp + 1 - 2 * core
    first_row = z * tok
    length = len_ref[0]
    rows_out = wg_ref.shape[0]
    split_seq = rows_out != depth

    def copy(source, target, send_sem, recv_sem, to_dp, to_z):
        return pltpu.make_async_remote_copy(
            src_ref=source, dst_ref=target, send_sem=send_sem, recv_sem=recv_sem,
            device_id=(to_dp, to_z), device_id_type=pl.DeviceIdType.MESH,
        )

    def columns(n):
        return pl.ds(pl.multiple_of(n * COLS, COLS), COLS)

    def same_core(d):
        return 2 * ring_add(chip, d, chips) + core

    def weight_copy(n, d):
        to = sibling if d == 0 else same_core(d)
        return copy(w_ref.at[:, columns(n)], w_all.at[n, dp], w_send.at[n, d], w_recv.at[n, dp], to, z)

    def weight_from(n, block, to):
        return copy(w_all.at[n, block], w_all.at[n, block], w_pass.at[n, 0], w_recv.at[n, block], to, z)

    def weight_pass(n, d):
        block = same_core(d)
        return copy(
            w_all.at[n, block], w_all.at[n, block], w_pass.at[n, d], w_recv.at[n, block], sibling, z
        )

    def halo_copy(n, side, s):
        ref = (k_hbm, v_hbm)[s]
        start = tok - HALF if side == 0 else 0
        return copy(
            ref.at[pl.ds(start, HALF), columns(n)], halo.at[side, s, n],
            halo_send.at[side, s, n], halo_recv.at[side, s, n], dp, z + 1 - 2 * side,
        )

    def rim_copy(n, side, s, hh):
        hc = pl.ds(hh * HEAD_DIM, HEAD_DIM)
        return copy(
            halo.at[side, s, n, :, hc], rim.at[1 - side, s, n, :, hc],
            rim_send.at[side, s, n, hh], rim_recv.at[1 - side, s, n, hh], dp, z - 1 + 2 * side,
        )

    def reduce_copy(s, n):
        bit = lax.rem(lax.div(dp, 2**s), 2)
        return copy(
            sends[s].at[n], recvs[s].at[n], red_send.at[s, n], red_recv.at[s, n],
            dp + (1 - 2 * bit) * 2**s, z,
        )

    def piece_copy(n, d):
        to = ring_add(z, d, seq)
        rows = pl.ds(pl.multiple_of(to * rows_out, 16), rows_out)
        return copy(
            piece.at[n, rows], piece_in.at[n, z], piece_send.at[n, d], piece_recv.at[n, z], dp, to
        )

    def piece_from(n, d):
        block = ring_add(z, d, seq)
        rows = pl.ds(pl.multiple_of(block * rows_out, 16), rows_out)
        return copy(
            piece.at[n, rows], piece_in.at[n, block], piece_send.at[n, d], piece_recv.at[n, block],
            dp, block,
        )

    def load(i):
        source = (go_hbm, q_hbm, k_hbm, v_hbm)[i]
        return pltpu.make_async_copy(source, (go_ref, q_ref, k_ref, v_ref)[i], load_sem.at[i])

    def weight_load(n):
        return pltpu.make_async_copy(w_ref.at[:, columns(n)], w_all.at[n, dp], weight_sem.at[n])

    def store(n, i):
        target = (gq_hbm, gk_hbm, gv_hbm)[i]
        return pltpu.make_async_copy(staged.at[i, n], target.at[:, columns(n)], store_sem.at[i, n])

    has_before, has_after = z > 0, z < seq - 1
    exists = (has_before, has_after)

    for i in range(4):
        load(i).start()
    barrier = pltpu.get_barrier_semaphore()
    peers = [(sibling, z)]
    peers += [(same_core(d), z) for d in range(1, chips)]
    peers += [(dp, ring_add(z, d, seq)) for d in range(1, seq)]
    for peer in peers:
        pl.semaphore_signal(barrier, inc=1, device_id=peer, device_id_type=pl.DeviceIdType.MESH)
    pl.semaphore_wait(barrier, len(peers))

    def begin(n):
        for d in range(chips):
            weight_copy(n, d).start()
        for side in range(2):
            @pl.when(exists[1 - side])
            def _():
                for s in range(2):
                    halo_copy(n, side, s).start()
        weight_load(n).start()

    begin(0)
    for side in range(2):
        @pl.when(jnp.logical_not(exists[side]))
        def _():
            halo[side] = jnp.zeros(halo.shape[1:], halo.dtype)

    fill_bias(bias, length, first_row)
    begin(1)
    load(0).wait()
    got[...] = go_ref[...].T
    begin(2)
    for i in range(1, 4):
        load(i).wait()

    def pass_weight(n):
        for d in range(1, chips):
            weight_from(n, same_core(d), sibling).wait_recv()
            weight_pass(n, d).start()

    def reduce_stage(s, n):
        slot = lax.rem(n, 2)
        if s > 0:
            reduce_copy(s - 1, n).wait_recv()

        def held(i):
            if s == 0:
                return part[i]
            return keeps[s - 1][slot, i] + recvs[s - 1][n, i].astype(jnp.float32)

        if s == stages:
            fin[n] = held(0)
            if split_seq:
                piece[n] = fin[n].astype(jnp.bfloat16)
                for d in range(1, seq):
                    piece_copy(n, d).start()
            return
        bit = lax.rem(lax.div(dp, 2**s), 2)
        for i in range(keeps[s].shape[1]):
            sends[s][n, i] = held(2 * i + 1 - bit).astype(jnp.bfloat16)
            keeps[s][slot, i] = held(2 * i + bit)
        reduce_copy(s, n).start()

    def stage_if(s, n):
        if s <= stages:
            @pl.when((n >= 0) & (n < groups))
            def _():
                reduce_stage(s, n)

    def even_stages(n):
        for s in range(stages - stages % 2, 1, -2):
            stage_if(s, n - s // 2)

    def odd_stages(n):
        for s in range(stages - 1 + stages % 2, 2, -2):
            stage_if(s, n - s // 2)

    def add_rims(n):
        for side in range(2):
            rows = pl.ds(0 if side == 0 else tok - HALF, HALF)

            @pl.when(exists[side])
            def _():
                for s in range(2):
                    for hh in range(GROUP):
                        rim_copy(n, 1 - side, s, hh).wait_recv()
                    own[s, n, rows] += rim[side, s, n].astype(jnp.float32)

        for s in range(2):
            staged[1 + s, n] = own[s, n].astype(jnp.bfloat16)
            store(n, 1 + s).start()

    pass_weight(0)

    def step(n, carry):
        cols = columns(n)
        for side in range(2):
            @pl.when(exists[side])
            def _():
                for s in range(2):
                    halo_copy(n, side, s).wait_recv()

        @pl.when(n + 3 < groups)
        def _():
            begin(n + 3)

        for s, (x, ref) in enumerate(((kx, k_ref), (vx, v_ref))):
            x[:HALF] = halo[0, s, n]
            x[HALF : HALF + tok] = ref[:, cols]
            x[HALF + tok :] = halo[1, s, n]
        chains = [(hh, i) for hh in range(GROUP) for i in range(tok // BLOCK)]
        for hh, i in chains:
            forward(hh, i, q_ref, cols, kx, vx, bias, prob, att, length, first_row)
        part[...] = mm(got[...], att[...], NT).reshape(part.shape)
        reduce_stage(0, n)
        even_stages(n)
        for d in range(chips):
            weight_from(n, same_core(d) + 1 - 2 * core, sibling).wait_recv()
        weight_load(n).wait()
        weight = w_all[n].reshape(count * depth, COLS)
        g[...] = mm(go_ref[...], weight, NN).astype(jnp.bfloat16)
        for c, (hh, i) in enumerate(chains):
            backward(hh, i, q_ref, cols, kx, vx, g, prob, staged, n, gk_acc, gv_acc)
            if c == 0:
                reduce_stage(1, n)
            if i == tok // BLOCK - 1:
                hc = slice(hh * HEAD_DIM, (hh + 1) * HEAD_DIM)
                for s, acc in enumerate((gk_acc, gv_acc)):
                    halo[0, s, n, :, hc] = acc[:HALF, hc].astype(jnp.bfloat16)
                    halo[1, s, n, :, hc] = acc[HALF + tok :, hc].astype(jnp.bfloat16)
                for side in range(2):
                    @pl.when(exists[side])
                    def _():
                        for s in range(2):
                            rim_copy(n, side, s, hh).start()
            if c == len(chains) // 2:
                odd_stages(n)
        store(n, 0).start()
        for s, acc in enumerate((gk_acc, gv_acc)):
            own[s, n] = acc[HALF : HALF + tok]

        @pl.when(n + 1 < groups)
        def _():
            pass_weight(n + 1)

        @pl.when(n >= 2)
        def _():
            add_rims(n - 2)

        return carry

    lax.fori_loop(0, groups, step, 0)

    for late in range((stages + 1) // 2):
        even_stages(groups + late)
        odd_stages(groups + late)

    def finish(n, carry):
        cols = columns(n)
        @pl.when(n >= groups - 2)
        def _():
            add_rims(n)

        if split_seq:
            total = fin[n, pl.ds(pl.multiple_of(z * rows_out, 16), rows_out)]
            for d in range(1, seq):
                piece_from(n, d).wait_recv()
                total += piece_in[n, ring_add(z, d, seq)].astype(jnp.float32)
            wg_ref[:, cols] = total
        else:
            wg_ref[:, cols] = fin[n]
        for i in range(3):
            store(n, i).wait()
        for d in range(chips):
            weight_copy(n, d).wait_send()
        for d in range(1, chips):
            weight_pass(n, d).wait_send()
        for side in range(2):
            @pl.when(exists[1 - side])
            def _():
                for s in range(2):
                    halo_copy(n, side, s).wait_send()

            @pl.when(exists[side])
            def _():
                for s in range(2):
                    for hh in range(GROUP):
                        rim_copy(n, side, s, hh).wait_send()
        for s in range(stages):
            reduce_copy(s, n).wait_send()
        if split_seq:
            for d in range(1, seq):
                piece_copy(n, d).wait_send()
        return carry

    lax.fori_loop(0, groups, finish, 0)


def copy_kernel(*refs):
    *refs, read_sem, write_sem = refs
    third = len(refs) // 3
    parts = []
    for i, (source, target, held) in enumerate(zip(refs[:third], refs[third : 2 * third], refs[2 * third :])):
        count = 4 if source.shape[0] % 64 == 0 else 1
        size = source.shape[0] // count
        for j in range(count):
            rows = pl.ds(j * size, size)
            parts.append(
                (
                    pltpu.make_async_copy(source.at[rows], held.at[rows], read_sem.at[i, j]),
                    pltpu.make_async_copy(held.at[rows], target.at[rows], write_sem.at[i, j]),
                )
            )
    for read, write in parts:
        read.start()
    for read, write in parts:
        read.wait()
        write.start()
    for read, write in parts:
        write.wait()


def handed_on(*arrays):
    hbm = pl.BlockSpec(memory_space=pl.ANY)
    return pl.pallas_call(
        copy_kernel,
        out_shape=[jax.ShapeDtypeStruct(x.shape, x.dtype) for x in arrays],
        in_specs=[hbm] * len(arrays),
        out_specs=[hbm] * len(arrays),
        scratch_shapes=[pltpu.VMEM(x.shape, x.dtype) for x in arrays]
        + [pltpu.SemaphoreType.DMA((len(arrays), 4))] * 2,
        compiler_params=pltpu.CompilerParams(vmem_limit_bytes=62 * 1024 * 1024),
    )(*arrays)


def shards(queries, keys, values, grad_out, out_weight, lengths):
    tok, width = queries.shape
    depth = out_weight.shape[0]
    count, seq = lax.axis_size("dp"), lax.axis_size("seq")
    stages = count.bit_length() - 1
    groups = width // COLS
    wide = tok + 2 * HALF
    split_seq = seq > 1 and (depth // seq) % 16 == 0
    rows_out = depth // seq if split_seq else depth
    vmem = pl.BlockSpec(memory_space=pltpu.VMEM)
    hbm = pl.BlockSpec(memory_space=pl.ANY)
    smem = pl.BlockSpec(memory_space=pltpu.SMEM)
    bf, f32 = jnp.bfloat16, jnp.float32
    dma = pltpu.SemaphoreType.DMA
    halves = [count >> (s + 1) for s in range(stages)]
    grad_query, grad_key, grad_value, weight_grad = pl.pallas_call(
        functools.partial(kernel, count, seq),
        out_shape=(
            jax.ShapeDtypeStruct((tok, width), bf),
            jax.ShapeDtypeStruct((tok, width), bf),
            jax.ShapeDtypeStruct((tok, width), bf),
            jax.ShapeDtypeStruct((rows_out, width), f32),
        ),
        in_specs=[smem] + [hbm] * 5,
        out_specs=(hbm, hbm, hbm, vmem),
        scratch_shapes=[
            pltpu.VMEM((tok, width), bf),
            pltpu.VMEM((tok, width), bf),
            pltpu.VMEM((tok, width), bf),
            pltpu.VMEM((tok, width), bf),
            dma((4,)),
            dma((groups,)),
            pltpu.VMEM((3, groups, tok, COLS), bf),
            dma((3, groups)),
            pltpu.VMEM((tok // BLOCK, BLOCK + 2 * HALF, BLOCK), f32),
            pltpu.VMEM((width, tok), bf),
            pltpu.VMEM((wide, COLS), bf),
            pltpu.VMEM((wide, COLS), bf),
            pltpu.VMEM((tok, COLS), bf),
            pltpu.VMEM((GROUP, tok // BLOCK, BLOCK + 2 * HALF, BLOCK), f32),
            pltpu.VMEM((COLS, tok), bf),
            pltpu.VMEM((wide, COLS), f32),
            pltpu.VMEM((wide, COLS), f32),
            pltpu.VMEM((groups, count, depth, COLS), bf),
            pltpu.VMEM((2, 2, groups, HALF, COLS), bf),
            pltpu.VMEM((2, 2, groups, HALF, COLS), bf),
            pltpu.VMEM((2, groups, tok, COLS), f32),
            pltpu.VMEM((count, depth, COLS), f32),
            pltpu.VMEM((groups, depth, COLS), f32),
            pltpu.VMEM((groups, depth, COLS), bf),
            pltpu.VMEM((groups, seq, depth // seq if split_seq else 16, COLS), bf),
            [pltpu.VMEM((2, h, depth, COLS), f32) for h in halves],
            [pltpu.VMEM((groups, h, depth, COLS), bf) for h in halves],
            [pltpu.VMEM((groups, h, depth, COLS), bf) for h in halves],
            dma((groups, count // 2)),
            dma((groups, count)),
            dma((groups, count // 2)),
            dma((2, 2, groups)),
            dma((2, 2, groups)),
            dma((2, 2, groups, GROUP)),
            dma((2, 2, groups, GROUP)),
            dma((stages, groups)),
            dma((stages, groups)),
            dma((groups, seq)),
            dma((groups, seq)),
        ],
        compiler_params=pltpu.CompilerParams(
            vmem_limit_bytes=62 * 1024 * 1024, collective_id=0, has_side_effects=True
        ),
        cost_estimate=pl.CostEstimate(
            flops=20_000_000_000, bytes_accessed=12_000_000, transcendentals=5_000_000
        ),
    )(lengths, queries, keys, values, grad_out, out_weight)
    if not split_seq:
        weight_grad = lax.psum_scatter(weight_grad, "seq", scatter_dimension=0, tiled=True)
    return handed_on(grad_query, grad_key, grad_value, weight_grad)


def solution(mesh):
    rows = P(("dp", "seq"), None)
    in_specs = (rows, rows, rows, rows, P("dp", None), P("dp"))
    return jax.shard_map(
        shards, mesh=mesh, in_specs=in_specs, out_specs=(rows,) * 4, check_vma=False
    )
```
